512 devices in a mesh: seq: 64 (over z, x), head: 8 (over y, core).
Axes of the slice: x: 4, y: 4, z: 16, core: 2. Of those that a mesh axis runs over, the one named last changes fastest.
Arguments:
- queries: bfloat16 [16384, 2048], P('seq', 'head'), may hold values from -6 to 6
- key_vectors: bfloat16 [16384, 2048], P('seq', 'head'), may hold values from -6 to 6
- value_vectors: bfloat16 [16384, 2048], P('seq', 'head'), may hold values from -6 to 6
- forget_gates: float32 [16384, 16], P('seq', 'head'), may hold values from 0.4 to 1, as said below
- shard_counts: int32 [64], P('seq'), may hold values from 1 to 256, 12288 in all
- gram_start: float32 [16, 128, 128], P('head'), may hold values from -4 to 12, as said below
- memory_start: float32 [16, 128, 128], P('head'), may hold values from -6 to 6
- ridge_terms: float32 [16, 128], P('head'), may hold values from 0.05 to 1
- norm_gain: float32 [2048], P('head'), may hold values from 0.1 to 1.9
- out_weight: bfloat16 [2048, 2048], P('head'), may hold values from -0.125 to 0.125
Outputs:
- mixed_out: bfloat16 [16384, 2048], P('seq', 'head')
The draws below stay inside these ranges and needn't reach their ends.
Inputs may be any that keep to these rules, and one draw needn't show every extreme that they name: `shard_counts`: slots of a shard at local positions from its count on are padding; at least one shard is full. `forget_gates`: each gate lies in (0, 1]. `gram_start`: each head's matrix is symmetric positive semidefinite.
All inputs are finite; a program needn't handle non-finite values.
Results may differ from the reference program's by a relative error of at most 0.02.
Values may be sent and summed in bfloat16 or wider, within the bound.
A program may use at most 64 MiB of HBM per device.

```python
import math
import jax
import jax.numpy as jnp
import numpy as np
from jax import lax

D = 2048
HEAD_COUNT = 16
HEAD_DIMENSION = 128
TOK_DEV = 256
ITERS = 16
TOKEN_SLOTS = 16384
N_SEQ = 64
N_HEAD = 8


def draw_gram_start(key, part):
    spanning_rows = jax.random.normal(key, (HEAD_COUNT, 4 * HEAD_DIMENSION, HEAD_DIMENSION), jnp.float32)
    return jnp.einsum('cgy,cgl->cyl', spanning_rows, spanning_rows, precision=lax.Precision.HIGHEST) / HEAD_DIMENSION


def head_order(head_key):
    return jax.random.permutation(head_key, HEAD_DIMENSION)


def draw_key_vectors(key, part):
    key_sequence = jax.random.split(key, 3)
    group_width = max(HEAD_DIMENSION // 8, 1)
    group_total = HEAD_DIMENSION // group_width
    orderings = jax.vmap(head_order)(jax.random.split(key_sequence[0], HEAD_COUNT))
    positions = jnp.argsort(orderings, axis=-1).astype(jnp.int32)
    group_index = positions // group_width
    head_offset = jax.random.randint(key_sequence[1], (HEAD_COUNT,), 0, group_total)
    shard_index = jnp.arange(TOKEN_SLOTS, dtype=jnp.int32) // TOK_DEV
    chosen_group = (shard_index[:, None] + head_offset[None, :]) % group_total
    favoured = group_index[None, :, :] == chosen_group[:, :, None]
    spread_scale = jnp.where(favoured, 1.5, 0.2)
    base_values = jax.random.normal(key_sequence[2], (TOKEN_SLOTS, HEAD_COUNT, HEAD_DIMENSION), jnp.float32)
    shaped = jnp.clip(base_values * spread_scale, -6.0, 6.0)
    return shaped.reshape(TOKEN_SLOTS, HEAD_COUNT * HEAD_DIMENSION).astype(jnp.bfloat16)


def draw_forget_gates(key, part):
    key_sequence = jax.random.split(key, 8)
    order_rank = jnp.argsort(jax.random.permutation(key_sequence[0], HEAD_COUNT)).astype(jnp.int32)
    slow_count = HEAD_COUNT // 2
    medium_count = 5 * HEAD_COUNT // 16
    slow_heads = order_rank < slow_count
    medium_heads = jnp.logical_and(order_rank >= slow_count, order_rank < slow_count + medium_count)
    fast_rate = jnp.exp(jax.random.uniform(key_sequence[1], (HEAD_COUNT,), jnp.float32, math.log(1.0 / 50.0), math.log(1.0 / 30.0)))
    slow_rate = jnp.exp(jax.random.uniform(key_sequence[2], (HEAD_COUNT,), jnp.float32, math.log(0.1), math.log(0.4))) / TOKEN_SLOTS
    medium_rate = jnp.exp(jax.random.uniform(key_sequence[7], (HEAD_COUNT,), jnp.float32, math.log(math.log(4.0)), math.log(math.log(10.0)))) / TOK_DEV
    per_head_rate = jnp.where(slow_heads, slow_rate, jnp.where(medium_heads, medium_rate, fast_rate))
    block_factor = jnp.exp(jax.random.uniform(key_sequence[3], (TOKEN_SLOTS // TOK_DEV, HEAD_COUNT), jnp.float32, math.log(0.5), math.log(2.0)))
    block_factor = jnp.repeat(block_factor, TOK_DEV, axis=0)
    small_perturbation = jax.random.uniform(key_sequence[4], (TOKEN_SLOTS, HEAD_COUNT), jnp.float32, 0.5, 1.5)
    marked_locations = jax.random.randint(key_sequence[5], (2, HEAD_COUNT), 0, TOKEN_SLOTS)
    token_place = jnp.arange(TOKEN_SLOTS, dtype=jnp.int32)
    spike_selected = jnp.any(token_place[:, None, None] == marked_locations[None, :, :], axis=1)
    spike_retain = jax.random.uniform(key_sequence[6], (TOKEN_SLOTS, HEAD_COUNT), jnp.float32, 0.5, 0.8)
    return jnp.exp(-per_head_rate[None, :] * block_factor * small_perturbation) * jnp.where(spike_selected, spike_retain, 1.0)


def level_of(key, dims, cuts, smallest, high):
    level = 1.0
    for dim, blocks in cuts:
        draws = jax.random.uniform(jax.random.fold_in(jax.random.fold_in(key, 6), dim), (blocks,), jnp.float32, smallest / len(cuts), high / len(cuts))
        level = level * jnp.repeat(jnp.exp(draws), dims[dim] // blocks).reshape((-1,) + (1,) * (len(dims) - 1 - dim))
    return level


def length_profile(count, total, bound, skew):
    loads = [(1 << 20) // math.isqrt(rank ** skew) + 1 for rank in range(2, count + 1)]
    spare, given = total - bound - (count - 1), [1] * (count - 1)
    while spare > 0:
        free = [i for i in range(count - 1) if given[i] < bound]
        whole, remaining = sum([loads[i] for i in free]), spare
        for i in free:
            addition = min(bound - given[i], max(1, remaining * loads[i] // whole), spare)
            given[i] = given[i] + addition
            spare = spare - addition
    return np.array([bound] + given)


def ragged(rng, number_of, total, limit, lean):
    if number_of == 2:
        one = jax.random.randint(rng, (), max(1, total - limit), min(limit, total - 1) + 1)
        return jnp.stack([one, total - one])
    sizes = jnp.asarray(length_profile(number_of, total, limit, lean), jnp.int32)
    couples = (number_of - 1) // 2
    donor, taker = sizes[1:1 + 2 * couples:2], sizes[2:2 + 2 * couples:2]
    slack = jnp.minimum(donor - 1, limit - taker)
    moved = jax.random.randint(jax.random.fold_in(rng, 1), (couples,), 0, 1 << 20) % (slack + 1)
    sizes = sizes.at[1:1 + 2 * couples:2].set(donor - moved).at[2:2 + 2 * couples:2].set(taker + moved)
    return sizes[jax.random.permutation(jax.random.fold_in(rng, 2), number_of)]


def gaussian(stream_key, extent, spread, most, cuts=(), kind=jnp.bfloat16):
    level = level_of(stream_key, extent, cuts, -0.22, 0.18) if cuts else 1.0
    values = jax.random.normal(stream_key, extent, jnp.float32) * spread * level
    return jnp.minimum(jnp.maximum(values, -most), most).astype(kind)


def setup_inputs(seed: int = 0) -> dict:
    seeds = jax.random.split(jax.random.key(seed), 11)
    return {
        "queries": gaussian(seeds[0], (TOKEN_SLOTS, HEAD_COUNT * HEAD_DIMENSION), 1.0, 6.0, ((0, 64), (1, 8))),
        "key_vectors": draw_key_vectors(jax.random.fold_in(seeds[10], 71), 0),
        "value_vectors": gaussian(seeds[2], (TOKEN_SLOTS, HEAD_COUNT * HEAD_DIMENSION), 1.0, 6.0, ((0, 64), (1, 8))),
        "forget_gates": draw_forget_gates(jax.random.fold_in(seeds[10], 71), 0),
        "shard_counts": ragged(seeds[4], N_SEQ, N_SEQ * TOK_DEV * 3 // 4, TOK_DEV, 0).astype(jnp.int32),
        "gram_start": draw_gram_start(jax.random.fold_in(seeds[10], 71), 0),
        "memory_start": gaussian(seeds[6], (HEAD_COUNT, HEAD_DIMENSION, HEAD_DIMENSION), 1.0, 6.0, ((0, 8),), jnp.float32),
        "ridge_terms": jnp.clip(jnp.exp(math.log(1.0) - 2.9957323 * jax.random.uniform(seeds[7], (HEAD_COUNT, HEAD_DIMENSION), jnp.float32) ** level_of(seeds[7], (HEAD_COUNT, HEAD_DIMENSION), ((0, 8),), -0.2, 0.2)), 0.05, 1.0),
        "norm_gain": jnp.clip(1.0 + 0.18 * jax.random.normal(seeds[8], (HEAD_COUNT * HEAD_DIMENSION,), jnp.float32), 0.1, 1.9),
        "out_weight": gaussian(seeds[9], (HEAD_COUNT * HEAD_DIMENSION, D), (HEAD_COUNT * HEAD_DIMENSION) ** -0.5, 0.125, ((0, 8),)),
    }


precise = lax.Precision.HIGHEST

def unit_rows(matrix):
    return matrix * lax.rsqrt(lax.optimization_barrier(jnp.sum(matrix * matrix, axis=-1, keepdims=True)) + 1e-06)

def summarize(key_rows, value_rows, running):
    tail_decay = jnp.exp(running[:, -1:] - running)[..., None]
    weighted = key_rows * tail_decay
    gram_local = jnp.einsum('hcd,hce->hde', weighted, key_rows, precision=precise)
    memory_local = jnp.einsum('hce,hcd->hed', value_rows, weighted, precision=precise)
    return (jnp.exp(running[:, -1]), gram_local, memory_local)

def solve_block(query_rows, key_rows, value_rows, running, gram_prev, memory_prev, ridge_terms):
    span_rows = running.shape[1]
    log_gaps = running[:, :, None] - running[:, None, :]
    lower_mask = lax.iota(jnp.int32, span_rows)[:, None] >= lax.iota(jnp.int32, span_rows)[None, :]
    within_block = jnp.where(lower_mask[None], jnp.exp(jnp.minimum(log_gaps, 0.0)), 0.0)
    lead_decay = jnp.exp(running)[..., None]
    ridge_diag = ridge_terms[:, None, :]

    def apply_op(vector_in, state_mat, rows_in):
        near_terms = jnp.einsum('hcd,hsd->hcs', vector_in, key_rows, precision=precise) * within_block
        return lead_decay * jnp.einsum('hcd,hed->hce', vector_in, state_mat, precision=precise) + jnp.einsum('hcs,hse->hce', near_terms, rows_in, precision=precise)

    def cg_step(loop_index, state_tuple):
        answer, residual, direction, norm_now = state_tuple
        image_vec = apply_op(direction, gram_prev, key_rows) + ridge_diag * direction
        step_size = norm_now / lax.optimization_barrier(jnp.sum(direction * image_vec, axis=-1, keepdims=True))
        answer = answer + step_size * direction
        residual = residual - step_size * image_vec
        norm_next = lax.optimization_barrier(jnp.sum(residual * residual, axis=-1, keepdims=True))
        direction = residual + norm_next / norm_now * direction
        return (answer, residual, direction, norm_next)
    initial = (jnp.zeros_like(query_rows), query_rows, query_rows, lax.optimization_barrier(jnp.sum(query_rows * query_rows, axis=-1, keepdims=True)))
    answer = lax.fori_loop(0, ITERS, cg_step, initial)[0]
    return apply_op(answer, memory_prev, value_rows)

def reference(queries, key_vectors, value_vectors, forget_gates, shard_counts, gram_start, memory_start, ridge_terms, norm_gain, out_weight):
    token_place = jnp.arange(TOKEN_SLOTS, dtype=jnp.int32)
    shard_of = (token_place // TOK_DEV).astype(jnp.int32)
    live_rows = (token_place % TOK_DEV < shard_counts[shard_of]).astype(jnp.float32)[:, None]

    def split_heads(matrix):
        return jnp.transpose(matrix.astype(jnp.float32).reshape(N_SEQ, TOK_DEV, HEAD_COUNT, HEAD_DIMENSION), (0, 2, 1, 3))
    live_blocks = live_rows.reshape(N_SEQ, 1, TOK_DEV, 1)
    query_rows = unit_rows(split_heads(queries))
    key_rows = unit_rows(split_heads(key_vectors)) * live_blocks
    value_rows = split_heads(value_vectors) * live_blocks
    log_decay = jnp.where(live_rows > 0, jnp.log(forget_gates), 0.0)
    log_decay = jnp.transpose(log_decay.reshape(N_SEQ, TOK_DEV, HEAD_COUNT), (0, 2, 1))
    running = jnp.cumsum(log_decay, axis=2)

    def shard_step(carried, inputs_now):
        gram_prev, memory_prev = carried
        query_block, key_block, value_block, running_block = inputs_now
        output = solve_block(query_block, key_block, value_block, running_block, gram_prev, memory_prev, ridge_terms)
        decay_total, gram_local, memory_local = summarize(key_block, value_block, running_block)
        gram_next = decay_total[:, None, None] * gram_prev + gram_local
        memory_next = decay_total[:, None, None] * memory_prev + memory_local
        return ((gram_next, memory_next), output)
    result = lax.scan(shard_step, (gram_start, memory_start), (query_rows, key_rows, value_rows, running))[1]
    scaled = result * lax.rsqrt(lax.optimization_barrier(jnp.mean(result * result, axis=-1, keepdims=True)) + 1e-05)
    flat_rows = jnp.transpose(scaled, (0, 2, 1, 3)).reshape(TOKEN_SLOTS, HEAD_COUNT * HEAD_DIMENSION) * norm_gain[None, :] * live_rows
    normalized = flat_rows.astype(jnp.bfloat16)
    group_width = HEAD_COUNT * HEAD_DIMENSION // N_HEAD
    mixed_sum = jnp.zeros((TOKEN_SLOTS, D), jnp.float32)
    for group_index in range(N_HEAD):
        lo_col = group_index * group_width
        partial_value = jnp.dot(normalized[:, lo_col:lo_col + group_width], out_weight[lo_col:lo_col + group_width], preferred_element_type=jnp.float32)
        rounded = lax.optimization_barrier(partial_value.astype(jnp.bfloat16))
        mixed_sum = mixed_sum + rounded.astype(jnp.float32)
    return mixed_sum.astype(jnp.bfloat16)
```

```python
import jax
import jax.numpy as jnp
from jax import lax
from jax.experimental import pallas as pl
from jax.experimental.pallas import tpu as pltpu
from jax.sharding import PartitionSpec as P

ITERS = 16
NZ, NX, NH = 16, 4, 8
T, DH = 256, 128
MESH = pl.DeviceIdType.MESH
F32, BF16 = jnp.float32, jnp.bfloat16
Z_ORDER = (8, 7, 9, 6, 10, 5, 11, 4, 12, 3, 13, 2, 14, 1, 15)


def dot(a, b):
    return jnp.dot(a, b, preferred_element_type=F32)


def two_parts(a):
    hi = a.astype(BF16)
    return hi, (a - hi.astype(F32)).astype(BF16)


def three_parts(a):
    hi = a.astype(BF16).astype(F32)
    mid = (a - hi).astype(BF16).astype(F32)
    return hi, mid, a - hi - mid


def kernel(
    cnt_ref, q_hbm, k_hbm, v_hbm, fg_hbm, gs_hbm, ms_hbm, rd_ref, ng_ref, ow_hbm, out_ref,
    qv, kv, vv, fg, st,
    xs, xr, part, zs, zr, zc, zg, xo, xg,
    kg, kt, vt, wk, wv, rb, lead_s, x_s, r_s, p_s,
    wcol, yg,
    lsem, xs_s, xs_r, zs_s, zs_r, zc_s, zc_r, xo_s, xo_r, w_s, w_r, y_s, y_r,
):
    seq = lax.axis_index("seq")
    me = lax.axis_index("head")
    z, x = lax.div(seq, NX), lax.rem(seq, NX)

    def x_peer(d):
        px = lax.rem(x + d, NX)
        return px, z * NX + px

    def z_peer(d):
        pz = lax.rem(z + d, NZ)
        return pz, pz * NX + x

    loads = [
        pltpu.make_async_copy(fg_hbm, fg, lsem.at[0]),
        pltpu.make_async_copy(k_hbm, kv, lsem.at[1]),
        pltpu.make_async_copy(v_hbm, vv, lsem.at[2]),
        pltpu.make_async_copy(q_hbm, qv, lsem.at[3]),
        pltpu.make_async_copy(gs_hbm, st.at[pl.ds(0, 2)], lsem.at[4]),
        pltpu.make_async_copy(ms_hbm, st.at[pl.ds(2, 2)], lsem.at[5]),
    ]
    for c in loads:
        c.start()
    w_own = pltpu.make_async_copy(
        ow_hbm.at[:, pl.ds(pl.multiple_of(me * T, T), T)], wcol.at[me], lsem.at[6]
    )
    w_own.start()

    barrier = pltpu.get_barrier_semaphore()
    for d in range(1, NX):
        pl.semaphore_signal(barrier, inc=1, device_id=(x_peer(d)[1], me), device_id_type=MESH)
    for d in range(1, NZ):
        pl.semaphore_signal(barrier, inc=1, device_id=(z_peer(d)[1], me), device_id_type=MESH)
    for d in range(1, NH):
        pl.semaphore_signal(
            barrier, inc=1, device_id=(seq, lax.rem(me + d, NH)), device_id_type=MESH
        )

    count = cnt_ref[0]
    live_col = (lax.broadcasted_iota(jnp.int32, (T, 1), 0) < count).astype(F32)
    live_row = (lax.broadcasted_iota(jnp.int32, (1, T), 1) < count).astype(F32)
    loads[0].wait()
    logs = jnp.where(live_col > 0, jnp.log(fg[...]), 0.0)
    lane = lax.broadcasted_iota(jnp.int32, (T, DH), 1)
    lmat = jnp.where(lane == 0, logs[:, 0:1], jnp.where(lane == 1, logs[:, 1:2], 0.0))
    rows8 = lmat.T[0:8]
    stacked = jnp.concatenate([*three_parts(rows8), jnp.zeros_like(rows8)], axis=0).astype(BF16)
    si = lax.broadcasted_iota(jnp.int32, (T, T + DH), 0)
    ti = lax.broadcasted_iota(jnp.int32, (T, T + DH), 1)
    upto = jnp.where(si <= ti, 1.0, 0.0).astype(BF16)
    sums = dot(stacked, upto)
    sums = sums[0:8] + sums[8:16] + sums[16:24]
    run_row, tot = sums[:, 0:T], sums[:, T:]
    run_col = jnp.concatenate([run_row, jnp.zeros((DH - 8, T), F32)], axis=0).T

    loads[1].wait()
    loads[2].wait()
    scale = []
    own = []
    for h in range(2):
        cols = slice(h * DH, (h + 1) * DH)
        kb = kv[:, cols]
        kf = kb.astype(F32)
        sc = lax.rsqrt(jnp.sum(kf * kf, axis=1, keepdims=True) + 1e-06) * live_col
        scale.append(sc)
        tail = jnp.exp(tot[h : h + 1, 0:1] - run_col[:, h : h + 1]) * sc
        wm = kf * tail
        wg_hi, wg_lo = two_parts(wm * sc)
        wm_hi, wm_lo = two_parts(wm)
        ktr = kf.T.astype(BF16)
        vtr = vv[:, cols].astype(F32).T.astype(BF16)
        kt[h] = jnp.concatenate([ktr, ktr], axis=1)
        vt[h] = vtr
        kg[h, 0:T] = jnp.concatenate([kb, kb], axis=1)
        own.append((dot(ktr, wg_hi) + dot(ktr, wg_lo), dot(vtr, wm_hi) + dot(vtr, wm_lo)))
    decay = jnp.concatenate([*three_parts(tot[0:2]), jnp.zeros((10, DH), F32)], axis=0).astype(BF16)
    for j in range(NX):
        rows = slice(32 * j, 32 * j + 32)
        xs[j, 0:DH] = jnp.concatenate(
            [own[0][0][rows], own[1][0][rows], own[0][1][rows], own[1][1][rows]], axis=0
        ).astype(BF16)
        xs[j, DH : DH + 16] = decay

    pl.semaphore_wait(barrier, NX + NZ + NH - 3)

    def x_send(d):
        px, dev = x_peer(d)
        return pltpu.make_async_remote_copy(
            xs.at[px], xr.at[x], xs_s.at[px], xs_r.at[x], device_id=(dev, me), device_id_type=MESH
        )

    def x_come(d):
        px, dev = x_peer(d)
        return pltpu.make_async_remote_copy(
            xr.at[px], xr.at[px], xs_s.at[px], xs_r.at[px], device_id=(dev, me), device_id_type=MESH
        )

    for d in (2, 1, 3):
        x_send(d).start()
    xr[x] = xs[x]

    loads[3].wait()
    rr0 = []
    for h in range(2):
        cols = slice(h * DH, (h + 1) * DH)
        decayed = jnp.where(
            si[:, 0:T] <= ti[:, 0:T],
            jnp.exp(jnp.minimum(run_row[h : h + 1] - run_col[:, h : h + 1], 0.0)),
            0.0,
        )
        wv_h = decayed * scale[h]
        wv[h] = wv_h
        wk[h] = wv_h * scale[h]
        lead_s[h] = jnp.exp(run_row[h : h + 1])
        ridge = jnp.broadcast_to(rd_ref[h : h + 1, :], (DH, DH)).T
        rb[h] = jnp.concatenate([ridge, ridge], axis=1)
        qt = qv[:, cols].astype(F32).T
        qn = qt * lax.rsqrt(jnp.sum(qt * qt, axis=0, keepdims=True) + 1e-06)
        x_s[h] = jnp.zeros_like(qn)
        r_s[h] = qn
        p_s[h] = qn
        rr0.append(jnp.sum(qn * qn, axis=0, keepdims=True))

    for d in (1, 3, 2):
        x_come(d).wait_recv()

    run = jnp.zeros((DH, DH), F32)
    four_log = jnp.zeros((2, DH), F32)
    lead_in = []

    def by_rows(pair):
        a = jnp.broadcast_to(pair[0:1], (32, DH))
        b = jnp.broadcast_to(pair[1:2], (32, DH))
        return jnp.concatenate([a, b, a, b], axis=0)

    for i in range(NX):
        part[i] = run
        lead_in.append(jnp.exp(four_log))
        d16 = xr[i, DH : DH + 16].astype(F32)
        log_i = d16[0:2] + d16[2:4] + d16[4:6]
        run = by_rows(jnp.exp(log_i)) * run + xr[i, 0:DH].astype(F32)
        four_log = four_log + log_i
    for j in range(NZ):
        hh = (j // 4) % 2
        zs[j] = jnp.concatenate(
            [run[8 * j : 8 * j + 8], *three_parts(four_log[hh : hh + 1]), jnp.zeros((5, DH), F32)],
            axis=0,
        ).astype(BF16)

    def z_send(d):
        pz, dev = z_peer(d)
        return pltpu.make_async_remote_copy(
            zs.at[pz], zr.at[z], zs_s.at[pz], zs_r.at[z], device_id=(dev, me), device_id_type=MESH
        )

    def z_come(d):
        pz, dev = z_peer(d)
        return pltpu.make_async_remote_copy(
            zr.at[pz], zr.at[pz], zs_s.at[pz], zs_r.at[pz], device_id=(dev, me), device_id_type=MESH
        )

    for d in Z_ORDER:
        z_send(d).start()
    zr[z] = zs[z]
    loads[4].wait()
    loads[5].wait()
    begin = pl.multiple_of(32 * x + 8 * lax.rem(z, 4), 8)
    carry = st[lax.div(z, 4), pl.ds(begin, 8), :]
    for d in reversed(Z_ORDER):
        z_come(d).wait_recv()
    for i in range(NZ):
        zc[i] = carry
        got = zr[i].astype(F32)
        carry = jnp.exp(got[8:9] + got[9:10] + got[10:11]) * carry + got[0:8]

    def c_send(d):
        pz, dev = z_peer(d)
        return pltpu.make_async_remote_copy(
            zc.at[pz], zg.at[z], zc_s.at[pz], zc_r.at[z], device_id=(dev, me), device_id_type=MESH
        )

    def c_come(d):
        pz, dev = z_peer(d)
        return pltpu.make_async_remote_copy(
            zg.at[pz], zg.at[pz], zc_s.at[pz], zc_r.at[pz], device_id=(dev, me), device_id_type=MESH
        )

    for d in Z_ORDER:
        c_send(d).start()
    zg[z] = zc[z]
    for d in reversed(Z_ORDER):
        c_come(d).wait_recv()

    carried = zg[...].reshape(DH, DH)
    for i in range(NX):
        xo[i] = (by_rows(lead_in[i]) * carried + part[i]).astype(BF16)

    def o_send(d):
        px, dev = x_peer(d)
        return pltpu.make_async_remote_copy(
            xo.at[px], xg.at[x], xo_s.at[px], xo_r.at[x], device_id=(dev, me), device_id_type=MESH
        )

    def o_come(d):
        px, dev = x_peer(d)
        return pltpu.make_async_remote_copy(
            xg.at[px], xg.at[px], xo_s.at[px], xo_r.at[px], device_id=(dev, me), device_id_type=MESH
        )

    for d in (2, 1, 3):
        o_send(d).start()
    xg[x] = xo[x]

    def w_send(d):
        ph = lax.rem(me + d, NH)
        return pltpu.make_async_remote_copy(
            ow_hbm.at[:, pl.ds(pl.multiple_of(ph * T, T), T)],
            wcol.at[me],
            w_s.at[ph],
            w_r.at[me],
            device_id=(seq, ph),
            device_id_type=MESH,
        )

    def w_come(d):
        ph = lax.rem(me + d, NH)
        return pltpu.make_async_remote_copy(
            wcol.at[ph], wcol.at[ph], w_s.at[ph], w_r.at[ph], device_id=(seq, ph), device_id_type=MESH
        )

    for d in range(1, NH):
        w_send(d).start()

    for d in (1, 3, 2):
        o_come(d).wait_recv()
    for h in range(2):
        for j in range(NX):
            gq = xg[j, 32 * h : 32 * h + 32]
            kg[h, T + 32 * j : T + 32 * j + 32] = jnp.concatenate([gq, gq], axis=1)

    def step(i, norms):
        after = []
        for h in range(2):
            p = p_s[h]
            u = dot(kg[h], jnp.concatenate(two_parts(p), axis=0))
            near = jnp.concatenate(two_parts(u[0:T] * wk[h]), axis=0)
            w = dot(kt[h], near) + lead_s[h] * u[T:] + rb[h] * p
            alpha = norms[h] / jnp.sum(p * w, axis=0, keepdims=True)
            x_s[h] += alpha * p
            r = r_s[h] - alpha * w
            r_s[h] = r
            new = jnp.sum(r * r, axis=0, keepdims=True)
            p_s[h] = r + (new / norms[h]) * p
            after.append(new)
        return tuple(after)

    lax.fori_loop(0, ITERS, step, tuple(rr0))

    ys = []
    for h in range(2):
        xb = x_s[h].astype(BF16)
        mem = jnp.concatenate([xg[j, 64 + 32 * h : 96 + 32 * h] for j in range(NX)], axis=0)
        near = (dot(kg[h, 0:T, 0:DH], xb) * wv[h]).astype(BF16)
        o = dot(vt[h], near) + lead_s[h] * dot(mem, xb)
        o = o * (lax.rsqrt(jnp.mean(o * o, axis=0, keepdims=True) + 1e-05) * live_row)
        ys.append(o.T * ng_ref[h : h + 1, :])
    yg[me] = jnp.concatenate(ys, axis=1).astype(BF16)

    def y_send(d):
        ph = lax.rem(me + d, NH)
        return pltpu.make_async_remote_copy(
            yg.at[me], yg.at[me], y_s.at[ph], y_r.at[me], device_id=(seq, ph), device_id_type=MESH
        )

    def y_come(d):
        ph = lax.rem(me + d, NH)
        return pltpu.make_async_remote_copy(
            yg.at[ph], yg.at[ph], y_s.at[ph], y_r.at[ph], device_id=(seq, ph), device_id_type=MESH
        )

    for d in range(1, NH):
        y_send(d).start()
    w_own.wait()
    acc = dot(yg[me], wcol[me]).astype(BF16).astype(F32)
    for d in range(1, NH):
        ph = lax.rem(me + d, NH)
        w_come(d).wait_recv()
        y_come(d).wait_recv()
        acc = acc + dot(yg[ph], wcol[ph]).astype(BF16).astype(F32)
    out_ref[...] = acc.astype(BF16)

    for d in range(1, NX):
        x_send(d).wait_send()
        o_send(d).wait_send()
    for d in range(1, NZ):
        z_send(d).wait_send()
        c_send(d).wait_send()
    for d in range(1, NH):
        w_send(d).wait_send()
        y_send(d).wait_send()


def local(q, k, v, fg, counts, gs, ms, ridge, gain, ow):
    vmem = pl.BlockSpec(memory_space=pltpu.VMEM)
    hbm = pl.BlockSpec(memory_space=pl.ANY)
    smem = pl.BlockSpec(memory_space=pltpu.SMEM)
    V, DMA = pltpu.VMEM, pltpu.SemaphoreType.DMA
    return pl.pallas_call(
        kernel,
        out_shape=jax.ShapeDtypeStruct((T, 2 * DH), BF16),
        in_specs=[smem, hbm, hbm, hbm, hbm, hbm, hbm, vmem, vmem, hbm],
        out_specs=vmem,
        scratch_shapes=[
            V((T, 2 * DH), BF16),
            V((T, 2 * DH), BF16),
            V((T, 2 * DH), BF16),
            V((T, 2), F32),
            V((4, DH, DH), F32),
            V((NX, DH + 16, DH), BF16),
            V((NX, DH + 16, DH), BF16),
            V((NX, DH, DH), F32),
            V((NZ, 16, DH), BF16),
            V((NZ, 16, DH), BF16),
            V((NZ, 8, DH), F32),
            V((NZ, 8, DH), F32),
            V((NX, DH, DH), BF16),
            V((NX, DH, DH), BF16),
            V((2, T + DH, 2 * DH), BF16),
            V((2, DH, 2 * T), BF16),
            V((2, DH, T), BF16),
            V((2, T, T), F32),
            V((2, T, T), F32),
            V((2, DH, T), F32),
            V((2, 1, T), F32),
            V((2, DH, T), F32),
            V((2, DH, T), F32),
            V((2, DH, T), F32),
            V((NH, T, 2 * DH), BF16),
            V((NH, T, 2 * DH), BF16),
            DMA((7,)),
            DMA((NX,)),
            DMA((NX,)),
            DMA((NZ,)),
            DMA((NZ,)),
            DMA((NZ,)),
            DMA((NZ,)),
            DMA((NX,)),
            DMA((NX,)),
            DMA((NH,)),
            DMA((NH,)),
            DMA((NH,)),
            DMA((NH,)),
        ],
        compiler_params=pltpu.CompilerParams(
            collective_id=0, has_side_effects=True, vmem_limit_bytes=48 * 1024 * 1024
        ),
        cost_estimate=pl.CostEstimate(
            flops=3_000_000_000, bytes_accessed=2_500_000, transcendentals=300_000
        ),
        name="mesa_layer",
    )(counts, q, k, v, fg, gs, ms, ridge, gain.reshape(2, DH), ow)


def solution(mesh):
    return jax.shard_map(
        local,
        mesh=mesh,
        in_specs=(
            P("seq", "head"),
            P("seq", "head"),
            P("seq", "head"),
            P("seq", "head"),
            P("seq"),
            P("head", None, None),
            P("head", None, None),
            P("head", None),
            P("head"),
            P("head", None),
        ),
        out_specs=P("seq", "head"),
        check_vma=False,
    )
```

```python
import jax
import jax.numpy as jnp
from jax import lax
from jax.experimental import pallas as pl
from jax.experimental.pallas import tpu as pltpu
from jax.sharding import PartitionSpec as P

ITERS = 16
NQ, NI, NX, NH = 4, 4, 4, 8
T, DH = 256, 128
MESH = pl.DeviceIdType.MESH
F32, BF16 = jnp.float32, jnp.bfloat16


def dot(a, b):
    return jnp.dot(a, b, preferred_element_type=F32)


def two_parts(a):
    hi = a.astype(BF16)
    return hi, (a - hi.astype(F32)).astype(BF16)


def three_parts(a):
    hi = a.astype(BF16).astype(F32)
    mid = (a - hi).astype(BF16).astype(F32)
    return hi, mid, a - hi - mid


def kernel(
    cnt_ref, q_hbm, k_hbm, v_hbm, fg_hbm, gs_hbm, ms_hbm, rd_ref, ng_ref, ow_hbm, out_ref,
    qv, kv, vv, fg, st,
    xs, xr, part, zs, zr, zpart, bs, br, begin_s, zc, zg, xo, xg,
    kg, kt, vt, wk, wv, rb, lead_s, x_s, r_s, p_s,
    wcol, yg,
    lsem, ready, xs_s, xs_r, zs_s, zs_r, bs_s, bs_r, zc_s, zc_r, xo_s, xo_r, w_s, w_r, y_s, y_r, f_s,
):
    seq = lax.axis_index("seq")
    me = lax.axis_index("head")
    z, x = lax.div(seq, NX), lax.rem(seq, NX)
    quad, idx = lax.div(z, NI), lax.rem(z, NI)

    def x_peer(d):
        px = lax.rem(x + d, NX)
        return px, z * NX + px

    def z_peer(d):
        pi = lax.rem(idx + d, NI)
        return pi, (quad * NI + pi) * NX + x

    def quad_at(pq):
        return (pq * NI + idx) * NX + x

    loads = [
        pltpu.make_async_copy(fg_hbm, fg, lsem.at[0]),
        pltpu.make_async_copy(k_hbm, kv, lsem.at[1]),
        pltpu.make_async_copy(v_hbm, vv, lsem.at[2]),
        pltpu.make_async_copy(q_hbm, qv, lsem.at[3]),
        pltpu.make_async_copy(gs_hbm, st.at[pl.ds(0, 2)], lsem.at[4]),
        pltpu.make_async_copy(ms_hbm, st.at[pl.ds(2, 2)], lsem.at[5]),
    ]
    for c in loads:
        c.start()
    w_own = pltpu.make_async_copy(
        ow_hbm.at[:, pl.ds(pl.multiple_of(me * T, T), T)], wcol.at[me], lsem.at[6]
    )
    w_own.start()

    barrier = pltpu.get_barrier_semaphore()
    for d in range(1, NX):
        pl.semaphore_signal(barrier, inc=1, device_id=(x_peer(d)[1], me), device_id_type=MESH)
    for d in range(1, NI):
        pl.semaphore_signal(barrier, inc=1, device_id=(z_peer(d)[1], me), device_id_type=MESH)
    for d in range(1, NH):
        pl.semaphore_signal(
            barrier, inc=1, device_id=(seq, lax.rem(me + d, NH)), device_id_type=MESH
        )
    for pq in range(1, NQ):

        @pl.when(pq > quad)
        def _():
            pl.semaphore_signal(barrier, inc=1, device_id=(quad_at(pq), me), device_id_type=MESH)

    count = cnt_ref[0]
    live_col = (lax.broadcasted_iota(jnp.int32, (T, 1), 0) < count).astype(F32)
    live_row = (lax.broadcasted_iota(jnp.int32, (1, T), 1) < count).astype(F32)
    loads[0].wait()
    logs = jnp.where(live_col > 0, jnp.log(fg[...]), 0.0)
    lane = lax.broadcasted_iota(jnp.int32, (T, DH), 1)
    lmat = jnp.where(lane == 0, logs[:, 0:1], jnp.where(lane == 1, logs[:, 1:2], 0.0))
    rows8 = lmat.T[0:8]
    stacked = jnp.concatenate([*three_parts(rows8), jnp.zeros_like(rows8)], axis=0).astype(BF16)
    si = lax.broadcasted_iota(jnp.int32, (T, T + DH), 0)
    ti = lax.broadcasted_iota(jnp.int32, (T, T + DH), 1)
    upto = jnp.where(si <= ti, 1.0, 0.0).astype(BF16)
    sums = dot(stacked, upto)
    sums = sums[0:8] + sums[8:16] + sums[16:24]
    run_row, tot = sums[:, 0:T], sums[:, T:]
    run_col = jnp.concatenate([run_row, jnp.zeros((DH - 8, T), F32)], axis=0).T

    loads[1].wait()
    loads[2].wait()
    scale = []
    own = []
    for h in range(2):
        cols = slice(h * DH, (h + 1) * DH)
        kb = kv[:, cols]
        kf = kb.astype(F32)
        sc = lax.rsqrt(jnp.sum(kf * kf, axis=1, keepdims=True) + 1e-06) * live_col
        scale.append(sc)
        tail = jnp.exp(tot[h : h + 1, 0:1] - run_col[:, h : h + 1]) * sc
        wm = kf * tail
        wg_hi, wg_lo = two_parts(wm * sc)
        wm_hi, wm_lo = two_parts(wm)
        ktr = kf.T.astype(BF16)
        vtr = vv[:, cols].astype(F32).T.astype(BF16)
        kt[h] = jnp.concatenate([ktr, ktr], axis=1)
        vt[h] = vtr
        kg[h, 0:T] = jnp.concatenate([kb, kb], axis=1)
        own.append((dot(ktr, wg_hi) + dot(ktr, wg_lo), dot(vtr, wm_hi) + dot(vtr, wm_lo)))
    decay = jnp.concatenate([*three_parts(tot[0:2]), jnp.zeros((10, DH), F32)], axis=0).astype(BF16)
    for j in range(NX):
        rows = slice(32 * j, 32 * j + 32)
        xs[j, 0:DH] = jnp.concatenate(
            [own[0][0][rows], own[1][0][rows], own[0][1][rows], own[1][1][rows]], axis=0
        ).astype(BF16)
        xs[j, DH : DH + 16] = decay

    pl.semaphore_wait(barrier, NX + NI + NH - 3 + quad)

    def x_send(d):
        px, dev = x_peer(d)
        return pltpu.make_async_remote_copy(
            xs.at[px], xr.at[x], xs_s.at[px], xs_r.at[x], device_id=(dev, me), device_id_type=MESH
        )

    def x_come(d):
        px, dev = x_peer(d)
        return pltpu.make_async_remote_copy(
            xr.at[px], xr.at[px], xs_s.at[px], xs_r.at[px], device_id=(dev, me), device_id_type=MESH
        )

    for d in (2, 1, 3):
        x_send(d).start()
    for pq in range(NQ - 1):

        @pl.when(pq < quad)
        def _():
            pl.semaphore_signal(
                ready.at[quad], inc=1, device_id=(quad_at(pq), me), device_id_type=MESH
            )

    xr[x] = xs[x]

    loads[3].wait()
    rr0 = []
    for h in range(2):
        cols = slice(h * DH, (h + 1) * DH)
        decayed = jnp.where(
            si[:, 0:T] <= ti[:, 0:T],
            jnp.exp(jnp.minimum(run_row[h : h + 1] - run_col[:, h : h + 1], 0.0)),
            0.0,
        )
        wv_h = decayed * scale[h]
        wv[h] = wv_h
        wk[h] = wv_h * scale[h]
        lead_s[h] = jnp.exp(run_row[h : h + 1])
        ridge = jnp.broadcast_to(rd_ref[h : h + 1, :], (DH, DH)).T
        rb[h] = jnp.concatenate([ridge, ridge], axis=1)
        qt = qv[:, cols].astype(F32).T
        qn = qt * lax.rsqrt(jnp.sum(qt * qt, axis=0, keepdims=True) + 1e-06)
        x_s[h] = jnp.zeros_like(qn)
        r_s[h] = qn
        p_s[h] = qn
        rr0.append(jnp.sum(qn * qn, axis=0, keepdims=True))

    for d in (1, 3, 2):
        x_come(d).wait_recv()

    run = jnp.zeros((DH, DH), F32)
    four_log = jnp.zeros((2, DH), F32)
    lead_in = []

    def by_rows(pair):
        a = jnp.broadcast_to(pair[0:1], (32, DH))
        b = jnp.broadcast_to(pair[1:2], (32, DH))
        return jnp.concatenate([a, b, a, b], axis=0)

    for i in range(NX):
        part[i] = run
        lead_in.append(jnp.exp(four_log))
        d16 = xr[i, DH : DH + 16].astype(F32)
        log_i = d16[0:2] + d16[2:4] + d16[4:6]
        run = by_rows(jnp.exp(log_i)) * run + xr[i, 0:DH].astype(F32)
        four_log = four_log + log_i
    def with_log(rows, log):
        return jnp.concatenate(
            [rows, *three_parts(log), jnp.zeros((13, DH), F32)], axis=0
        ).astype(BF16)

    def parts_of(got):
        tail = got[32:48].astype(F32)
        return got[0:32].astype(F32), tail[0:1] + tail[1:2] + tail[2:3]

    for j in range(NI):
        zs[j] = with_log(run[32 * j : 32 * j + 32], four_log[j % 2 : j % 2 + 1])

    def z_send(d):
        pi, dev = z_peer(d)
        return pltpu.make_async_remote_copy(
            zs.at[pi], zr.at[idx], zs_s.at[pi], zs_r.at[idx], device_id=(dev, me), device_id_type=MESH
        )

    def z_come(d):
        pi, dev = z_peer(d)
        return pltpu.make_async_remote_copy(
            zr.at[pi], zr.at[pi], zs_s.at[pi], zs_r.at[pi], device_id=(dev, me), device_id_type=MESH
        )

    for d in (2, 3, 1):
        z_send(d).start()
    zr[idx] = zs[idx]
    for d in (1, 3, 2):
        z_come(d).wait_recv()

    run = jnp.zeros((32, DH), F32)
    quad_log = jnp.zeros((1, DH), F32)
    quad_in = []
    for k in range(NI):
        zpart[k] = run
        quad_in.append(jnp.exp(quad_log))
        rows, log_k = parts_of(zr[k])
        run = jnp.exp(log_k) * run + rows
        quad_log = quad_log + log_k
    bs[...] = with_log(run, quad_log)

    def b_send(pq):
        return pltpu.make_async_remote_copy(
            bs, br.at[quad], bs_s.at[pq], bs_r.at[quad], device_id=(quad_at(pq), me), device_id_type=MESH
        )

    def b_come(pq):
        return pltpu.make_async_remote_copy(
            br.at[pq], br.at[pq], bs_s.at[pq], bs_r.at[pq], device_id=(quad_at(pq), me), device_id_type=MESH
        )

    for pq in range(1, NQ):

        @pl.when(pq > quad)
        def _():
            pl.semaphore_wait(ready.at[pq], 1)
            b_send(pq).start()

    loads[4].wait()
    loads[5].wait()
    begin_s[...] = st[idx, pl.ds(pl.multiple_of(32 * x, 32), 32), :]
    for pq in range(NQ - 1):

        @pl.when(pq < quad)
        def _():
            b_come(pq).wait_recv()
            rows, log_q = parts_of(br[pq])
            begin_s[...] = jnp.exp(log_q) * begin_s[...] + rows

    for k in range(NI):
        zc[k] = (quad_in[k] * begin_s[...] + zpart[k]).astype(BF16)

    def c_send(d):
        pi, dev = z_peer(d)
        return pltpu.make_async_remote_copy(
            zc.at[pi], zg.at[idx], zc_s.at[pi], zc_r.at[idx], device_id=(dev, me), device_id_type=MESH
        )

    def c_come(d):
        pi, dev = z_peer(d)
        return pltpu.make_async_remote_copy(
            zg.at[pi], zg.at[pi], zc_s.at[pi], zc_r.at[pi], device_id=(dev, me), device_id_type=MESH
        )

    for d in (2, 3, 1):
        c_send(d).start()
    zg[idx] = zc[idx]
    for d in (1, 3, 2):
        c_come(d).wait_recv()

    carried = jnp.concatenate([zg[k].astype(F32) for k in range(NI)], axis=0)
    for i in range(NX):
        xo[i] = (by_rows(lead_in[i]) * carried + part[i]).astype(BF16)

    def o_send(d):
        px, dev = x_peer(d)
        return pltpu.make_async_remote_copy(
            xo.at[px], xg.at[x], xo_s.at[px], xo_r.at[x], device_id=(dev, me), device_id_type=MESH
        )

    def o_come(d):
        px, dev = x_peer(d)
        return pltpu.make_async_remote_copy(
            xg.at[px], xg.at[px], xo_s.at[px], xo_r.at[px], device_id=(dev, me), device_id_type=MESH
        )

    for d in (2, 1, 3):
        o_send(d).start()
    xg[x] = xo[x]

    def w_send(d):
        ph = lax.rem(me + d, NH)
        return pltpu.make_async_remote_copy(
            ow_hbm.at[:, pl.ds(pl.multiple_of(ph * T, T), T)],
            wcol.at[me],
            w_s.at[ph],
            w_r.at[me],
            device_id=(seq, ph),
            device_id_type=MESH,
        )

    def w_come(d):
        ph = lax.rem(me + d, NH)
        return pltpu.make_async_remote_copy(
            wcol.at[ph], wcol.at[ph], w_s.at[ph], w_r.at[ph], device_id=(seq, ph), device_id_type=MESH
        )

    for d in range(1, NH):
        w_send(d).start()

    for d in (1, 3, 2):
        o_come(d).wait_recv()
    for h in range(2):
        for j in range(NX):
            gq = xg[j, 32 * h : 32 * h + 32]
            kg[h, T + 32 * j : T + 32 * j + 32] = jnp.concatenate([gq, gq], axis=1)

    def step(i, norms):
        after = []
        for h in range(2):
            p = p_s[h]
            u = dot(kg[h], jnp.concatenate(two_parts(p), axis=0))
            near = jnp.concatenate(two_parts(u[0:T] * wk[h]), axis=0)
            w = dot(kt[h], near) + lead_s[h] * u[T:] + rb[h] * p
            alpha = norms[h] / jnp.sum(p * w, axis=0, keepdims=True)
            x_s[h] += alpha * p
            r = r_s[h] - alpha * w
            r_s[h] = r
            new = jnp.sum(r * r, axis=0, keepdims=True)
            p_s[h] = r + (new / norms[h]) * p
            after.append(new)
        return tuple(after)

    lax.fori_loop(0, ITERS, step, tuple(rr0))

    ys = []
    for h in range(2):
        xb = x_s[h].astype(BF16)
        mem = jnp.concatenate([xg[j, 64 + 32 * h : 96 + 32 * h] for j in range(NX)], axis=0)
        near = (dot(kg[h, 0:T, 0:DH], xb) * wv[h]).astype(BF16)
        o = dot(vt[h], near) + lead_s[h] * dot(mem, xb)
        o = o * (lax.rsqrt(jnp.mean(o * o, axis=0, keepdims=True) + 1e-05) * live_row)
        ys.append(o.T * ng_ref[h : h + 1, :])
    yg[me] = jnp.concatenate(ys, axis=1).astype(BF16)

    mate = me + 1 - 2 * lax.rem(me, 2)

    def y_copy(slot, to):
        return pltpu.make_async_remote_copy(
            yg.at[slot], yg.at[slot], y_s.at[to], y_r.at[slot], device_id=(seq, to), device_id_type=MESH
        )

    def y_on(slot):
        return pltpu.make_async_remote_copy(
            yg.at[slot], yg.at[slot], f_s.at[slot], y_r.at[slot], device_id=(seq, mate), device_id_type=MESH
        )

    far = [lax.rem(me + d, NH) for d in (4, 2, 6)]
    for to in far:
        y_copy(me, to).start()
    y_copy(me, mate).start()
    w_own.wait()
    for d in range(1, NH):
        w_come(d).wait_recv()

    def product(slot):
        return dot(yg[slot], wcol[slot]).astype(BF16).astype(F32)

    acc = product(me)
    y_copy(mate, mate).wait_recv()
    acc = acc + product(mate)
    order = [far[1], far[2], far[0]]
    for slot in order:
        y_copy(slot, slot).wait_recv()
        y_on(slot).start()
        acc = acc + product(slot)
    for slot in order:
        other = slot + mate - me
        y_copy(other, mate).wait_recv()
        acc = acc + product(other)
    out_ref[...] = acc.astype(BF16)

    for d in range(1, NX):
        x_send(d).wait_send()
        o_send(d).wait_send()
    for d in range(1, NI):
        z_send(d).wait_send()
        c_send(d).wait_send()
    for pq in range(1, NQ):

        @pl.when(pq > quad)
        def _():
            b_send(pq).wait_send()

    for d in range(1, NH):
        w_send(d).wait_send()
    y_copy(me, mate).wait_send()
    for slot in far:
        y_copy(me, slot).wait_send()
        y_on(slot).wait_send()


def local(q, k, v, fg, counts, gs, ms, ridge, gain, ow):
    vmem = pl.BlockSpec(memory_space=pltpu.VMEM)
    hbm = pl.BlockSpec(memory_space=pltpu.HBM)
    smem = pl.BlockSpec(memory_space=pltpu.SMEM)
    V, DMA = pltpu.VMEM, pltpu.SemaphoreType.DMA
    return pl.pallas_call(
        kernel,
        out_shape=jax.ShapeDtypeStruct((T, 2 * DH), BF16),
        in_specs=[smem, hbm, hbm, hbm, hbm, hbm, hbm, vmem, vmem, hbm],
        out_specs=vmem,
        scratch_shapes=[
            V((T, 2 * DH), BF16),
            V((T, 2 * DH), BF16),
            V((T, 2 * DH), BF16),
            V((T, 2), F32),
            V((4, DH, DH), F32),
            V((NX, DH + 16, DH), BF16),
            V((NX, DH + 16, DH), BF16),
            V((NX, DH, DH), F32),
            V((NI, 48, DH), BF16),
            V((NI, 48, DH), BF16),
            V((NI, 32, DH), F32),
            V((48, DH), BF16),
            V((NQ, 48, DH), BF16),
            V((32, DH), F32),
            V((NI, 32, DH), BF16),
            V((NI, 32, DH), BF16),
            V((NX, DH, DH), BF16),
            V((NX, DH, DH), BF16),
            V((2, T + DH, 2 * DH), BF16),
            V((2, DH, 2 * T), BF16),
            V((2, DH, T), BF16),
            V((2, T, T), F32),
            V((2, T, T), F32),
            V((2, DH, T), F32),
            V((2, 1, T), F32),
            V((2, DH, T), F32),
            V((2, DH, T), F32),
            V((2, DH, T), F32),
            V((NH, T, 2 * DH), BF16),
            V((NH, T, 2 * DH), BF16),
            DMA((7,)),
            pltpu.SemaphoreType.REGULAR((NQ,)),
            DMA((NX,)),
            DMA((NX,)),
            DMA((NI,)),
            DMA((NI,)),
            DMA((NQ,)),
            DMA((NQ,)),
            DMA((NI,)),
            DMA((NI,)),
            DMA((NX,)),
            DMA((NX,)),
            DMA((NH,)),
            DMA((NH,)),
            DMA((NH,)),
            DMA((NH,)),
            DMA((NH,)),
        ],
        compiler_params=pltpu.CompilerParams(
            collective_id=0, has_side_effects=True, vmem_limit_bytes=48 * 1024 * 1024
        ),
        cost_estimate=pl.CostEstimate(
            flops=3_000_000_000, bytes_accessed=2_500_000, transcendentals=300_000
        ),
        name="mesa_layer",
    )(counts, q, k, v, fg, gs, ms, ridge, gain.reshape(2, DH), ow)


def solution(mesh):
    return jax.shard_map(
        local,
        mesh=mesh,
        in_specs=(
            P("seq", "head"),
            P("seq", "head"),
            P("seq", "head"),
            P("seq", "head"),
            P("seq"),
            P("head", None, None),
            P("head", None, None),
            P("head", None),
            P("head"),
            P("head", None),
        ),
        out_specs=P("seq", "head"),
        check_vma=False,
    )
```

```python
import jax
import jax.numpy as jnp
from jax import lax
from jax.experimental import pallas as pl
from jax.experimental.pallas import tpu as pltpu
from jax.sharding import PartitionSpec as P

ITERS = 16
NQ, NI, NX, NH = 4, 4, 4, 8
T, DH = 256, 128
MESH = pl.DeviceIdType.MESH
F32, BF16 = jnp.float32, jnp.bfloat16


def dot(a, b):
    return jnp.dot(a, b, preferred_element_type=F32)


def two_parts(a):
    hi = a.astype(BF16)
    return hi, (a - hi.astype(F32)).astype(BF16)


def three_parts(a):
    hi = a.astype(BF16).astype(F32)
    mid = (a - hi).astype(BF16).astype(F32)
    return hi, mid, a - hi - mid


def kernel(
    cnt_hbm, q_hbm, k_hbm, v_hbm, fg_hbm, gs_hbm, ms_hbm, rd_hbm, ng_hbm, ow_hbm, out_ref,
    cnt_ref, rd_ref, ng_ref, qv, kv, vv, fg, st,
    xs, xr, xsm, xrm, part, zs, zr, zsm, zrm, zpart, bs, br, bsm, brm, begin_s, zc, zg, zcm, zgm, xo, xg, xom, xgm,
    kg, kt, vt, wk, wv, rb, lead_s, x_s, r_s, p_s,
    wcol, yg, acc_s,
    lsem, ready, x_sem, z_sem, b_sem, c_sem, o_sem, w_s, w_r, y_s, y_r,
):
    seq = lax.axis_index("seq")
    me = lax.axis_index("head")
    z, x = lax.div(seq, NX), lax.rem(seq, NX)
    quad, idx = lax.div(z, NI), lax.rem(z, NI)

    def x_peer(d):
        px = lax.rem(x + d, NX)
        return px, z * NX + px

    def z_peer(d):
        pi = lax.rem(idx + d, NI)
        return pi, (quad * NI + pi) * NX + x

    def quad_at(pq):
        return (pq * NI + idx) * NX + x

    loads = [
        pltpu.make_async_copy(fg_hbm, fg, lsem.at[0]),
        pltpu.make_async_copy(k_hbm, kv, lsem.at[1]),
        pltpu.make_async_copy(v_hbm, vv, lsem.at[2]),
        pltpu.make_async_copy(q_hbm, qv, lsem.at[3]),
        pltpu.make_async_copy(gs_hbm, st.at[pl.ds(0, 2)], lsem.at[4]),
        pltpu.make_async_copy(ms_hbm, st.at[pl.ds(2, 2)], lsem.at[5]),
        pltpu.make_async_copy(cnt_hbm, cnt_ref, lsem.at[7]),
        pltpu.make_async_copy(rd_hbm, rd_ref, lsem.at[8]),
        pltpu.make_async_copy(ng_hbm, ng_ref, lsem.at[9]),
    ]
    for c in loads:
        c.start()
    w_own = pltpu.make_async_copy(
        ow_hbm.at[:, pl.ds(pl.multiple_of(me * T, T), T)], wcol.at[me], lsem.at[6]
    )
    w_own.start()

    barrier = pltpu.get_barrier_semaphore()
    for d in range(1, NX):
        pl.semaphore_signal(barrier, inc=1, device_id=(x_peer(d)[1], me), device_id_type=MESH)
    for d in range(1, NI):
        pl.semaphore_signal(barrier, inc=1, device_id=(z_peer(d)[1], me), device_id_type=MESH)
    for d in range(1, NH):
        pl.semaphore_signal(
            barrier, inc=1, device_id=(seq, lax.rem(me + d, NH)), device_id_type=MESH
        )
    for pq in range(1, NQ):

        @pl.when(pq > quad)
        def _():
            pl.semaphore_signal(barrier, inc=1, device_id=(quad_at(pq), me), device_id_type=MESH)

    for c in (loads[6], loads[7], loads[8], loads[0]):
        c.wait()
    count = cnt_ref[0]
    live_col = (lax.broadcasted_iota(jnp.int32, (T, 1), 0) < count).astype(F32)
    live_row = (lax.broadcasted_iota(jnp.int32, (1, T), 1) < count).astype(F32)
    logs = jnp.where(live_row > 0, jnp.log(fg[...]), 0.0)
    rows8 = jnp.concatenate([logs, jnp.zeros((6, T), F32)], axis=0)
    stacked = jnp.concatenate([*three_parts(rows8), jnp.zeros_like(rows8)], axis=0).astype(BF16)
    si = lax.broadcasted_iota(jnp.int32, (T, T + DH), 0)
    ti = lax.broadcasted_iota(jnp.int32, (T, T + DH), 1)
    upto = jnp.where(si <= ti, 1.0, 0.0).astype(BF16)
    sums = dot(stacked, upto)
    sums = sums[0:8] + sums[8:16] + sums[16:24]
    run_row, tot = sums[:, 0:T], sums[:, T:]
    run_col = jnp.concatenate([run_row, jnp.zeros((DH - 8, T), F32)], axis=0).T

    loads[1].wait()
    scale = []
    weighted = []
    own = []
    for h in range(2):
        cols = slice(h * DH, (h + 1) * DH)
        kb = kv[:, cols]
        kf = kb.astype(F32)
        sc = lax.rsqrt(jnp.sum(kf * kf, axis=1, keepdims=True) + 1e-06) * live_col
        scale.append(sc)
        wm = kf * (jnp.exp(tot[h : h + 1, 0:1] - run_col[:, h : h + 1]) * sc)
        weighted.append(wm)
        wg_hi, wg_lo = two_parts(wm * sc)
        ktr = kf.T.astype(BF16)
        kt[h] = jnp.concatenate([ktr, ktr], axis=1)
        kg[h, 0:T] = jnp.concatenate([kb, kb], axis=1)
        own.append(dot(ktr, wg_hi) + dot(ktr, wg_lo))
    decay = jnp.concatenate([*three_parts(tot[0:2]), jnp.zeros((10, DH), F32)], axis=0).astype(BF16)
    for j in range(NX):
        rows = slice(32 * j, 32 * j + 32)
        xs[j, 0:64] = jnp.concatenate([own[0][rows], own[1][rows]], axis=0).astype(BF16)
        xs[j, 64:80] = decay

    pl.semaphore_wait(barrier, NX + NI + NH - 3 + quad)

    def swap(src, dst, sem, pair, to, here):
        def send():
            return pltpu.make_async_remote_copy(
                src.at[to], dst.at[here], sem.at[0, to], sem.at[1, here],
                device_id=(pair, me), device_id_type=MESH,
            )

        def come():
            return pltpu.make_async_remote_copy(
                dst.at[to], dst.at[to], sem.at[0, to], sem.at[1, to],
                device_id=(pair, me), device_id_type=MESH,
            )

        return send, come

    def along_x(src, dst, sem):
        return [swap(src, dst, sem, x_peer(d)[1], x_peer(d)[0], x) for d in (2, 1, 3)]

    def along_z(src, dst, sem):
        return [swap(src, dst, sem, z_peer(d)[1], z_peer(d)[0], idx) for d in (2, 3, 1)]

    def start(pairs):
        for send, _ in pairs:
            send().start()

    def arrive(pairs):
        for _, come in reversed(pairs):
            come().wait_recv()

    xg_pairs, xm_pairs = along_x(xs, xr, x_sem.at[0]), along_x(xsm, xrm, x_sem.at[1])
    start(xg_pairs)
    for pq in range(NQ - 1):

        @pl.when(pq < quad)
        def _():
            pl.semaphore_signal(
                ready.at[quad], inc=1, device_id=(quad_at(pq), me), device_id_type=MESH
            )

    xr[x] = xs[x]
    loads[2].wait()
    own = []
    for h in range(2):
        cols = slice(h * DH, (h + 1) * DH)
        wm_hi, wm_lo = two_parts(weighted[h])
        vtr = vv[:, cols].astype(F32).T.astype(BF16)
        vt[h] = vtr
        own.append(dot(vtr, wm_hi) + dot(vtr, wm_lo))
    for j in range(NX):
        rows = slice(32 * j, 32 * j + 32)
        xsm[j] = jnp.concatenate([own[0][rows], own[1][rows]], axis=0).astype(BF16)
    start(xm_pairs)
    xrm[x] = xsm[x]

    def w_send(d):
        ph = lax.rem(me + d, NH)
        return pltpu.make_async_remote_copy(
            ow_hbm.at[:, pl.ds(pl.multiple_of(ph * T, T), T)],
            wcol.at[me],
            w_s.at[ph],
            w_r.at[me],
            device_id=(seq, ph),
            device_id_type=MESH,
        )

    def w_come(d):
        ph = lax.rem(me + d, NH)
        return pltpu.make_async_remote_copy(
            wcol.at[ph], wcol.at[ph], w_s.at[ph], w_r.at[ph], device_id=(seq, ph), device_id_type=MESH
        )

    for d in range(1, NH):
        w_send(d).start()

    loads[3].wait()
    rr0 = []
    for h in range(2):
        cols = slice(h * DH, (h + 1) * DH)
        decayed = jnp.where(
            si[:, 0:T] <= ti[:, 0:T],
            jnp.exp(jnp.minimum(run_row[h : h + 1] - run_col[:, h : h + 1], 0.0)),
            0.0,
        )
        wv_h = decayed * scale[h]
        wv[h] = wv_h
        wk[h] = wv_h * scale[h]
        lead_s[h] = jnp.exp(run_row[h : h + 1])
        ridge = jnp.broadcast_to(rd_ref[h : h + 1, :], (DH, DH)).T
        rb[h] = jnp.concatenate([ridge, ridge], axis=1)
        qt = qv[:, cols].astype(F32).T
        qn = qt * lax.rsqrt(jnp.sum(qt * qt, axis=0, keepdims=True) + 1e-06)
        x_s[h] = jnp.zeros_like(qn)
        r_s[h] = qn
        p_s[h] = qn
        rr0.append(jnp.sum(qn * qn, axis=0, keepdims=True))

    def by_rows(pair):
        return jnp.concatenate(
            [jnp.broadcast_to(pair[0:1], (32, DH)), jnp.broadcast_to(pair[1:2], (32, DH))], axis=0
        )

    def with_log(rows, log):
        return jnp.concatenate([rows, *three_parts(log), jnp.zeros((13, DH), F32)], axis=0).astype(BF16)

    def log_in(tail):
        tail = tail.astype(F32)
        return tail[0:1] + tail[1:2] + tail[2:3]

    arrive(xg_pairs)
    logs_x = []
    for i in range(NX):
        d16 = xr[i, 64:80].astype(F32)
        logs_x.append(d16[0:2] + d16[2:4] + d16[4:6])
    lead_in = [jnp.zeros((2, DH), F32)]
    for i in range(NX):
        lead_in.append(lead_in[i] + logs_x[i])
    four_log = lead_in[NX]

    def in_four(which, got):
        run = jnp.zeros((64, DH), F32)
        for i in range(NX):
            part[which, i] = run
            run = by_rows(jnp.exp(logs_x[i])) * run + got[i, 0:64].astype(F32)
        return run

    run = in_four(0, xr)
    for j in range(NI):
        zs[j] = with_log(run[16 * j : 16 * j + 16], four_log[j // 2 : j // 2 + 1])
    zg_pairs, zm_pairs = along_z(zs, zr, z_sem.at[0]), along_z(zsm, zrm, z_sem.at[1])
    start(zg_pairs)
    zr[idx] = zs[idx]

    arrive(xm_pairs)
    run = in_four(1, xrm)
    for j in range(NI):
        zsm[j] = run[16 * j : 16 * j + 16].astype(BF16)
    start(zm_pairs)
    zrm[idx] = zsm[idx]

    def b_copies(src, dst, sem):
        def send(pq):
            return pltpu.make_async_remote_copy(
                src, dst.at[quad], sem.at[0, pq], sem.at[1, quad],
                device_id=(quad_at(pq), me), device_id_type=MESH,
            )

        def come(pq):
            return pltpu.make_async_remote_copy(
                dst.at[pq], dst.at[pq], sem.at[0, pq], sem.at[1, pq],
                device_id=(quad_at(pq), me), device_id_type=MESH,
            )

        return send, come

    bg_send, bg_come = b_copies(bs, br, b_sem.at[0])
    bm_send, bm_come = b_copies(bsm, brm, b_sem.at[1])

    def in_quad(which, got, logs_z):
        run = jnp.zeros((16, DH), F32)
        for k in range(NI):
            zpart[which, k] = run
            run = jnp.exp(logs_z[k]) * run + got[k, 0:16].astype(F32)
        return run

    begin_row = pl.multiple_of(32 * x + 16 * lax.rem(idx, 2), 16)

    arrive(zg_pairs)
    logs_z = [log_in(zr[k, 16:32]) for k in range(NI)]
    quad_in = [jnp.zeros((1, DH), F32)]
    for k in range(NI):
        quad_in.append(quad_in[k] + logs_z[k])
    bs[...] = with_log(in_quad(0, zr, logs_z), quad_in[NI])
    for pq in range(1, NQ):

        @pl.when(pq > quad)
        def _():
            pl.semaphore_wait(ready.at[pq], 1)
            bg_send(pq).start()

    loads[4].wait()
    loads[5].wait()
    begin_s[0] = st[lax.div(idx, 2), pl.ds(begin_row, 16), :]
    begin_s[1] = st[2 + lax.div(idx, 2), pl.ds(begin_row, 16), :]
    for pq in range(NQ - 1):

        @pl.when(pq < quad)
        def _():
            bg_come(pq).wait_recv()
            begin_s[0] = jnp.exp(log_in(br[pq, 16:32])) * begin_s[0] + br[pq, 0:16].astype(F32)

    for k in range(NI):
        zc[k] = (jnp.exp(quad_in[k]) * begin_s[0] + zpart[0, k]).astype(BF16)
    cg_pairs, cm_pairs = along_z(zc, zg, c_sem.at[0]), along_z(zcm, zgm, c_sem.at[1])
    start(cg_pairs)
    zg[idx] = zc[idx]

    arrive(zm_pairs)
    bsm[...] = in_quad(1, zrm, logs_z).astype(BF16)
    for pq in range(1, NQ):

        @pl.when(pq > quad)
        def _():
            bm_send(pq).start()

    def finish(which, carried, out):
        base = jnp.concatenate([carried[k].astype(F32) for k in range(NI)], axis=0)
        for i in range(NX):
            out[i] = (by_rows(jnp.exp(lead_in[i])) * base + part[which, i]).astype(BF16)

    arrive(cg_pairs)
    finish(0, zg, xo)
    og_pairs, om_pairs = along_x(xo, xg, o_sem.at[0]), along_x(xom, xgm, o_sem.at[1])
    start(og_pairs)
    xg[x] = xo[x]

    for pq in range(NQ - 1):

        @pl.when(pq < quad)
        def _():
            bm_come(pq).wait_recv()
            begin_s[1] = jnp.exp(log_in(br[pq, 16:32])) * begin_s[1] + brm[pq].astype(F32)

    for k in range(NI):
        zcm[k] = (jnp.exp(quad_in[k]) * begin_s[1] + zpart[1, k]).astype(BF16)
    start(cm_pairs)
    zgm[idx] = zcm[idx]

    arrive(og_pairs)
    for h in range(2):
        for j in range(NX):
            gq = xg[j, 32 * h : 32 * h + 32]
            kg[h, T + 32 * j : T + 32 * j + 32] = jnp.concatenate([gq, gq], axis=1)

    def memory_home():
        arrive(cm_pairs)
        finish(1, zgm, xom)
        start(om_pairs)
        xgm[x] = xom[x]

    def step(i, norms):
        ps = [p_s[h] for h in range(2)]
        us = [dot(kg[h], jnp.concatenate(two_parts(ps[h]), axis=0)) for h in range(2)]
        nears = [jnp.concatenate(two_parts(us[h][0:T] * wk[h]), axis=0) for h in range(2)]
        ws = [dot(kt[h], nears[h]) for h in range(2)]
        ws = [ws[h] + (lead_s[h] * us[h][T:] + rb[h] * ps[h]) for h in range(2)]
        alphas = [norms[h] / jnp.sum(ps[h] * ws[h], axis=0, keepdims=True) for h in range(2)]
        after = []
        for h in range(2):
            x_s[h] += alphas[h] * ps[h]
            r = r_s[h] - alphas[h] * ws[h]
            r_s[h] = r
            new = jnp.sum(r * r, axis=0, keepdims=True)
            p_s[h] = r + (new / norms[h]) * ps[h]
            after.append(new)
        return tuple(after)

    norms = lax.fori_loop(0, 4, step, tuple(rr0))
    memory_home()
    lax.fori_loop(4, ITERS, step, norms)
    arrive(om_pairs)

    core = lax.rem(me, 2)
    mate = me + 1 - 2 * core
    plus, minus, far = lax.rem(me + 2, NH), lax.rem(me + 6, NH), lax.rem(me + 4, NH)
    half = T // 2

    def y_copy(c, slot, to, n):
        here = yg.at[slot, pl.ds(c * half, half)]
        return pltpu.make_async_remote_copy(
            here, here, y_s.at[c, n], y_r.at[c, slot], device_id=(seq, to), device_id_type=MESH
        )

    mem = [jnp.concatenate([xgm[j, 32 * h : 32 * h + 32] for j in range(NX)], axis=0) for h in range(2)]
    xb = [x_s[h].astype(BF16) for h in range(2)]
    near = [(dot(kg[h, 0:T, 0:DH], xb[h]) * wv[h]).astype(BF16) for h in range(2)]
    o = [dot(vt[h], near[h]) + lead_s[h] * dot(mem[h], xb[h]) for h in range(2)]
    o = [
        a * (lax.rsqrt(jnp.mean(a * a, axis=0, keepdims=True) + 1e-05) * live_row) for a in o
    ]
    for c in range(2):
        rows = slice(c * half, c * half + half)
        yg[me, rows] = jnp.concatenate(
            [o[h][:, rows].T * ng_ref[h : h + 1, :] for h in range(2)], axis=1
        ).astype(BF16)
        y_copy(c, me, plus, 0).start()
        y_copy(c, me, minus, 1).start()
        y_copy(c, me, mate, 2).start()
    w_own.wait()
    for d in range(1, NH):
        w_come(d).wait_recv()

    acc_s[...] = dot(yg[me], wcol[me]).astype(BF16).astype(F32)

    def add(c, slot):
        rows = slice(c * half, c * half + half)
        acc_s[rows] += dot(yg[slot, rows], wcol[slot]).astype(BF16).astype(F32)

    first = jnp.where(core == 0, minus, plus)
    second = jnp.where(core == 0, plus, minus)
    for c in range(2):
        y_copy(c, first, mate, 3).wait_recv()
        y_copy(c, first, second, 3).start()
        y_copy(c, first, mate, 4).start()
        y_copy(c, second, mate, 5).wait_recv()
        y_copy(c, second, mate, 5).start()
        if c == 0:
            for b in range(2):
                y_copy(b, mate, mate, 2).wait_recv()
                add(b, mate)
        add(c, first)
        add(c, second)
    for c in range(2):
        y_copy(c, far, mate, 6).wait_recv()
        y_copy(c, far, mate, 6).start()
        for slot in (second, first):
            other = slot + mate - me
            y_copy(c, other, mate, 5).wait_recv()
            add(c, other)
        add(c, far)
    for c in range(2):
        other = far + mate - me
        y_copy(c, other, mate, 6).wait_recv()
        add(c, other)
    out_ref[...] = acc_s[...].astype(BF16)

    for pairs in (
        xg_pairs, xm_pairs, zg_pairs, zm_pairs, cg_pairs, cm_pairs, og_pairs, om_pairs,
    ):
        for send, _ in pairs:
            send().wait_send()
    for pq in range(1, NQ):

        @pl.when(pq > quad)
        def _():
            bg_send(pq).wait_send()
            bm_send(pq).wait_send()

    for d in range(1, NH):
        w_send(d).wait_send()
    for c in range(2):
        for n in range(7):
            y_copy(c, me, mate, n).wait_send()


def local(q, k, v, fg, counts, gs, ms, ridge, gain, ow):
    vmem = pl.BlockSpec(memory_space=pltpu.VMEM)
    hbm = pl.BlockSpec(memory_space=pltpu.HBM)
    V, DMA = pltpu.VMEM, pltpu.SemaphoreType.DMA
    return pl.pallas_call(
        kernel,
        out_shape=jax.ShapeDtypeStruct((T, 2 * DH), BF16),
        in_specs=[hbm] * 10,
        out_specs=vmem,
        scratch_shapes=[
            pltpu.SMEM((1,), jnp.int32),
            V((2, DH), F32),
            V((2, DH), F32),
            V((T, 2 * DH), BF16),
            V((T, 2 * DH), BF16),
            V((T, 2 * DH), BF16),
            V((2, T), F32),
            V((4, DH, DH), F32),
            V((NX, 80, DH), BF16),
            V((NX, 80, DH), BF16),
            V((NX, 64, DH), BF16),
            V((NX, 64, DH), BF16),
            V((2, NX, 64, DH), F32),
            V((NI, 32, DH), BF16),
            V((NI, 32, DH), BF16),
            V((NI, 16, DH), BF16),
            V((NI, 16, DH), BF16),
            V((2, NI, 16, DH), F32),
            V((32, DH), BF16),
            V((NQ, 32, DH), BF16),
            V((16, DH), BF16),
            V((NQ, 16, DH), BF16),
            V((2, 16, DH), F32),
            V((NI, 16, DH), BF16),
            V((NI, 16, DH), BF16),
            V((NI, 16, DH), BF16),
            V((NI, 16, DH), BF16),
            V((NX, 64, DH), BF16),
            V((NX, 64, DH), BF16),
            V((NX, 64, DH), BF16),
            V((NX, 64, DH), BF16),
            V((2, T + DH, 2 * DH), BF16),
            V((2, DH, 2 * T), BF16),
            V((2, DH, T), BF16),
            V((2, T, T), F32),
            V((2, T, T), F32),
            V((2, DH, T), F32),
            V((2, 1, T), F32),
            V((2, DH, T), F32),
            V((2, DH, T), F32),
            V((2, DH, T), F32),
            V((NH, T, 2 * DH), BF16),
            V((NH, T, 2 * DH), BF16),
            V((T, 2 * DH), F32),
            DMA((10,)),
            pltpu.SemaphoreType.REGULAR((NQ,)),
            DMA((2, 2, NX)),
            DMA((2, 2, NI)),
            DMA((2, 2, NQ)),
            DMA((2, 2, NI)),
            DMA((2, 2, NX)),
            DMA((NH,)),
            DMA((NH,)),
            DMA((2, 7)),
            DMA((2, NH)),
        ],
        compiler_params=pltpu.CompilerParams(
            collective_id=0, has_side_effects=True, vmem_limit_bytes=63 * 1024 * 1024
        ),
        cost_estimate=pl.CostEstimate(
            flops=3_000_000_000, bytes_accessed=2_500_000, transcendentals=300_000
        ),
        name="mesa_layer",
    )(counts, q, k, v, fg.T, gs, ms, ridge, gain.reshape(2, DH), ow)


def solution(mesh):
    return jax.shard_map(
        local,
        mesh=mesh,
        in_specs=(
            P("seq", "head"),
            P("seq", "head"),
            P("seq", "head"),
            P("seq", "head"),
            P("seq"),
            P("head", None, None),
            P("head", None, None),
            P("head", None),
            P("head"),
            P("head", None),
        ),
        out_specs=P("seq", "head"),
        check_vma=False,
    )
```

```python
import jax
import jax.numpy as jnp
from jax import lax
from jax.experimental import pallas as pl
from jax.experimental.pallas import tpu as pltpu
from jax.sharding import PartitionSpec as P

ITERS = 16
NQ, NG, NX, NH = 4, 16, 4, 8
T, DH = 256, 128
MESH = pl.DeviceIdType.MESH
F32, BF16 = jnp.float32, jnp.bfloat16


def dot(a, b):
    return jnp.dot(a, b, preferred_element_type=F32)


def two_parts(a):
    hi = a.astype(BF16)
    return hi, (a - hi.astype(F32)).astype(BF16)


def three_parts(a):
    hi = a.astype(BF16).astype(F32)
    mid = (a - hi).astype(BF16).astype(F32)
    return hi, mid, a - hi - mid


def kernel(
    cnt_hbm, q_hbm, k_hbm, v_hbm, fg_hbm, gs_hbm, ms_hbm, rd_hbm, ng_hbm, ow_hbm, out_ref,
    cnt_ref, rd_ref, ng_ref, qv, kv, vv, fg, st,
    xs, xr, xsm, xrm, part, bs, br, bt, bu, xo, xg, xom, xgm,
    kg, kt, vt, wk, wv, rb, lead_s, x_s, r_s, p_s,
    wcol, yg, acc_s,
    lsem, ready, x_sem, b_sem, o_sem, w_s, w_r, y_s, y_r, f_s,
):
    seq = lax.axis_index("seq")
    me = lax.axis_index("head")
    quad, mine = lax.div(seq, NG), lax.rem(seq, NG)

    def peer(dz, dx):
        other = lax.rem(lax.div(mine, NX) + dz, NX) * NX + lax.rem(lax.rem(mine, NX) + dx, NX)
        return other, quad * NG + other

    steps = [(dz, dx) for dz in (2, 3, 1, 0) for dx in (2, 1, 3, 0)][:-1]

    above, below = seq + NG, seq - NG

    loads = [
        pltpu.make_async_copy(fg_hbm, fg, lsem.at[0]),
        pltpu.make_async_copy(k_hbm, kv, lsem.at[1]),
        pltpu.make_async_copy(v_hbm, vv, lsem.at[2]),
        pltpu.make_async_copy(q_hbm, qv, lsem.at[3]),
        pltpu.make_async_copy(gs_hbm, st.at[pl.ds(0, 2)], lsem.at[4]),
        pltpu.make_async_copy(ms_hbm, st.at[pl.ds(2, 2)], lsem.at[5]),
        pltpu.make_async_copy(cnt_hbm, cnt_ref, lsem.at[7]),
        pltpu.make_async_copy(rd_hbm, rd_ref, lsem.at[8]),
        pltpu.make_async_copy(ng_hbm, ng_ref, lsem.at[9]),
    ]
    for c in loads:
        c.start()
    w_own = pltpu.make_async_copy(
        ow_hbm.at[:, pl.ds(pl.multiple_of(me * T, T), T)], wcol.at[me], lsem.at[6]
    )
    w_own.start()

    barrier = pltpu.get_barrier_semaphore()
    for dz, dx in steps:
        pl.semaphore_signal(barrier, inc=1, device_id=(peer(dz, dx)[1], me), device_id_type=MESH)
    for d in range(1, NH):
        pl.semaphore_signal(
            barrier, inc=1, device_id=(seq, lax.rem(me + d, NH)), device_id_type=MESH
        )

    @pl.when(quad < NQ - 1)
    def _():
        pl.semaphore_signal(barrier, inc=1, device_id=(above, me), device_id_type=MESH)

    @pl.when(quad == 1)
    def _():
        pl.semaphore_signal(barrier, inc=1, device_id=(seq + 2 * NG, me), device_id_type=MESH)

    for c in (loads[6], loads[7], loads[8], loads[0]):
        c.wait()
    count = cnt_ref[0]
    live_col = (lax.broadcasted_iota(jnp.int32, (T, 1), 0) < count).astype(F32)
    live_row = (lax.broadcasted_iota(jnp.int32, (1, T), 1) < count).astype(F32)
    logs = jnp.where(live_row > 0, jnp.log(fg[...]), 0.0)
    rows8 = jnp.concatenate([logs, jnp.zeros((6, T), F32)], axis=0)
    stacked = jnp.concatenate([*three_parts(rows8), jnp.zeros_like(rows8)], axis=0).astype(BF16)
    si = lax.broadcasted_iota(jnp.int32, (T, T + DH), 0)
    ti = lax.broadcasted_iota(jnp.int32, (T, T + DH), 1)
    upto = jnp.where(si <= ti, 1.0, 0.0).astype(BF16)
    sums = dot(stacked, upto)
    sums = sums[0:8] + sums[8:16] + sums[16:24]
    run_row, tot = sums[:, 0:T], sums[:, T:]
    run_col = jnp.concatenate([run_row, jnp.zeros((DH - 8, T), F32)], axis=0).T

    loads[1].wait()
    scale = []
    weighted = []
    own = []
    for h in range(2):
        cols = slice(h * DH, (h + 1) * DH)
        kb = kv[:, cols]
        kf = kb.astype(F32)
        sc = lax.rsqrt(jnp.sum(kf * kf, axis=1, keepdims=True) + 1e-06) * live_col
        scale.append(sc)
        wm = kf * (jnp.exp(tot[h : h + 1, 0:1] - run_col[:, h : h + 1]) * sc)
        weighted.append(wm)
        wg_hi, wg_lo = two_parts(wm * sc)
        ktr = kf.T.astype(BF16)
        kt[h] = jnp.concatenate([ktr, ktr], axis=1)
        kg[h, 0:T] = jnp.concatenate([kb, kb], axis=1)
        own.append(dot(ktr, wg_hi) + dot(ktr, wg_lo))
    for j in range(NG):
        h, at = j // 8, 16 * (j % 8)
        xs[j] = jnp.concatenate(
            [own[h][at : at + 16], *three_parts(tot[h : h + 1]), jnp.zeros((13, DH), F32)], axis=0
        ).astype(BF16)

    pl.semaphore_wait(barrier, NG + NH - 2 + jnp.minimum(quad, 1) + lax.div(quad, 3))

    def swap(src, dst, sem, pair, to, here):
        def send():
            return pltpu.make_async_remote_copy(
                src.at[to], dst.at[here], sem.at[0, to], sem.at[1, here],
                device_id=(pair, me), device_id_type=MESH,
            )

        def come():
            return pltpu.make_async_remote_copy(
                dst.at[to], dst.at[to], sem.at[0, to], sem.at[1, to],
                device_id=(pair, me), device_id_type=MESH,
            )

        return send, come

    def around(src, dst, sem):
        return [swap(src, dst, sem, dev, other, mine) for other, dev in (peer(*d) for d in steps)]

    def start(pairs):
        for send, _ in pairs:
            send().start()

    def arrive(pairs):
        for _, come in reversed(pairs):
            come().wait_recv()

    xg_pairs, xm_pairs = around(xs, xr, x_sem.at[0]), around(xsm, xrm, x_sem.at[1])
    start(xg_pairs)

    @pl.when(quad > 0)
    def _():
        pl.semaphore_signal(ready.at[0], inc=1, device_id=(below, me), device_id_type=MESH)

    @pl.when(quad == 3)
    def _():
        pl.semaphore_signal(ready.at[1], inc=1, device_id=(seq - 2 * NG, me), device_id_type=MESH)

    xr[mine] = xs[mine]
    loads[2].wait()
    own = []
    for h in range(2):
        cols = slice(h * DH, (h + 1) * DH)
        wm_hi, wm_lo = two_parts(weighted[h])
        vtr = vv[:, cols].astype(F32).T.astype(BF16)
        vt[h] = vtr
        own.append(dot(vtr, wm_hi) + dot(vtr, wm_lo))
    for j in range(NG):
        at = 16 * (j % 8)
        xsm[j] = own[j // 8][at : at + 16].astype(BF16)
    start(xm_pairs)
    xrm[mine] = xsm[mine]

    def w_send(d):
        ph = lax.rem(me + d, NH)
        return pltpu.make_async_remote_copy(
            ow_hbm.at[:, pl.ds(pl.multiple_of(ph * T, T), T)],
            wcol.at[me],
            w_s.at[ph],
            w_r.at[me],
            device_id=(seq, ph),
            device_id_type=MESH,
        )

    def w_come(d):
        ph = lax.rem(me + d, NH)
        return pltpu.make_async_remote_copy(
            wcol.at[ph], wcol.at[ph], w_s.at[ph], w_r.at[ph], device_id=(seq, ph), device_id_type=MESH
        )

    for d in range(1, NH):
        w_send(d).start()

    loads[3].wait()
    rr0 = []
    for h in range(2):
        cols = slice(h * DH, (h + 1) * DH)
        decayed = jnp.where(
            si[:, 0:T] <= ti[:, 0:T],
            jnp.exp(jnp.minimum(run_row[h : h + 1] - run_col[:, h : h + 1], 0.0)),
            0.0,
        )
        wv_h = decayed * scale[h]
        wv[h] = wv_h
        wk[h] = wv_h * scale[h]
        lead_s[h] = jnp.exp(run_row[h : h + 1])
        ridge = jnp.broadcast_to(rd_ref[h : h + 1, :], (DH, DH)).T
        rb[h] = jnp.concatenate([ridge, ridge], axis=1)
        qt = qv[:, cols].astype(F32).T
        qn = qt * lax.rsqrt(jnp.sum(qt * qt, axis=0, keepdims=True) + 1e-06)
        x_s[h] = jnp.zeros_like(qn)
        r_s[h] = qn
        p_s[h] = qn
        rr0.append(jnp.sum(qn * qn, axis=0, keepdims=True))

    def log_in(tail):
        tail = tail.astype(F32)
        return tail[0:1] + tail[1:2] + tail[2:3]

    def b_copy(which, n, to):
        src, dst = (bt, bu) if n == 2 else (bs, br)
        return pltpu.make_async_remote_copy(
            src.at[which], dst.at[which], b_sem.at[which, n], b_sem.at[which, 3 + n // 2],
            device_id=(to, me), device_id_type=MESH,
        )

    def b_next(which):
        return b_copy(which, 0, above)

    def b_skip(which):
        return b_copy(which, 1, seq + 2 * NG)

    def b_sum(which):
        return b_copy(which, 2, above)

    def in_quad(which, got):
        run = jnp.zeros((16, DH), F32)
        for k in range(NG):
            part[which, k] = run
            run = jnp.exp(logs[k]) * run + got[k, 0:16].astype(F32)
        return run

    head = lax.div(mine, 8)
    begin_row = pl.multiple_of(16 * lax.rem(mine, 8), 16)

    arrive(xg_pairs)
    logs = [log_in(xr[k, 16:32]) for k in range(NG)]
    lead_in = [jnp.zeros((1, DH), F32)]
    for k in range(NG):
        lead_in.append(lead_in[k] + logs[k])
    loads[4].wait()
    loads[5].wait()
    starts = (st[head, pl.ds(begin_row, 16), :], st[2 + head, pl.ds(begin_row, 16), :])

    def enter(which, got):
        total = in_quad(which, got)

        @pl.when(quad == 0)
        def _():
            br[which] = starts[which]

        @pl.when(quad == 2)
        def _():
            bt[which, 0:16] = total
            bt[which, 16:24] = jnp.broadcast_to(lead_in[NG], (8, DH))
            if which == 0:
                pl.semaphore_wait(ready.at[0], 1)
            b_sum(which).start()

        @pl.when(quad > 0)
        def _():
            b_next(which).wait_recv()

        @pl.when(quad == 3)
        def _():
            b_sum(which).wait_recv()
            br[which] = jnp.exp(bu[which, 16:17]) * br[which] + bu[which, 0:16]

        carry = br[which]

        @pl.when(quad < 2)
        def _():
            bs[which] = jnp.exp(lead_in[NG]) * carry + total

        @pl.when(quad == 1)
        def _():
            if which == 0:
                pl.semaphore_wait(ready.at[0], 1)
            b_next(which).start()
            if which == 0:
                pl.semaphore_wait(ready.at[1], 1)
            b_skip(which).start()

        return carry

    def finish(which, carry, out):
        for k in range(NG):
            out[k] = (jnp.exp(lead_in[k]) * carry + part[which, k]).astype(BF16)

    carry = enter(0, xr)

    finish(0, carry, xo)
    og_pairs, om_pairs = around(xo, xg, o_sem.at[0]), around(xom, xgm, o_sem.at[1])
    start(og_pairs)
    xg[mine] = xo[mine]

    @pl.when(quad == 0)
    def _():
        pl.semaphore_wait(ready.at[0], 1)
        b_next(0).start()

    arrive(xm_pairs)
    carry = enter(1, xrm)

    @pl.when(quad == 0)
    def _():
        b_next(1).start()

    finish(1, carry, xom)
    start(om_pairs)
    xgm[mine] = xom[mine]

    arrive(og_pairs)
    for h in range(2):
        g = xg[8 * h : 8 * h + 8].reshape(DH, DH)
        kg[h, T:] = jnp.concatenate([g, g], axis=1)

    def step(i, norms):
        ps = [p_s[h] for h in range(2)]
        us = [dot(kg[h], jnp.concatenate(two_parts(ps[h]), axis=0)) for h in range(2)]
        nears = [jnp.concatenate(two_parts(us[h][0:T] * wk[h]), axis=0) for h in range(2)]
        ws = [dot(kt[h], nears[h]) for h in range(2)]
        ws = [ws[h] + (lead_s[h] * us[h][T:] + rb[h] * ps[h]) for h in range(2)]
        alphas = [norms[h] / jnp.sum(ps[h] * ws[h], axis=0, keepdims=True) for h in range(2)]
        after = []
        for h in range(2):
            x_s[h] += alphas[h] * ps[h]
            r = r_s[h] - alphas[h] * ws[h]
            r_s[h] = r
            new = jnp.sum(r * r, axis=0, keepdims=True)
            p_s[h] = r + (new / norms[h]) * ps[h]
            after.append(new)
        return tuple(after)

    lax.fori_loop(0, ITERS, step, tuple(rr0))
    arrive(om_pairs)

    ys = []
    for h in range(2):
        xb = x_s[h].astype(BF16)
        mem = xgm[8 * h : 8 * h + 8].reshape(DH, DH)
        near = (dot(kg[h, 0:T, 0:DH], xb) * wv[h]).astype(BF16)
        o = dot(vt[h], near) + lead_s[h] * dot(mem, xb)
        o = o * (lax.rsqrt(jnp.mean(o * o, axis=0, keepdims=True) + 1e-05) * live_row)
        ys.append(o.T * ng_ref[h : h + 1, :])
    yg[me] = jnp.concatenate(ys, axis=1).astype(BF16)

    mate = me + 1 - 2 * lax.rem(me, 2)

    def y_copy(slot, to):
        return pltpu.make_async_remote_copy(
            yg.at[slot], yg.at[slot], y_s.at[to], y_r.at[slot], device_id=(seq, to), device_id_type=MESH
        )

    def y_on(slot):
        return pltpu.make_async_remote_copy(
            yg.at[slot], yg.at[slot], f_s.at[slot], y_r.at[slot], device_id=(seq, mate), device_id_type=MESH
        )

    far = [lax.rem(me + d, NH) for d in (4, 2, 6)]
    for to in far:
        y_copy(me, to).start()
    y_copy(me, mate).start()
    w_own.wait()
    for d in range(1, NH):
        w_come(d).wait_recv()

    def product(slot):
        return dot(yg[slot], wcol[slot]).astype(BF16).astype(F32)

    acc = product(me)
    y_copy(mate, mate).wait_recv()
    acc = acc + product(mate)
    order = [far[1], far[2], far[0]]
    for slot in order:
        y_copy(slot, slot).wait_recv()
        y_on(slot).start()
        acc = acc + product(slot)
    for slot in order:
        other = slot + mate - me
        y_copy(other, mate).wait_recv()
        acc = acc + product(other)
    out_ref[...] = acc.astype(BF16)

    for pairs in (
        xg_pairs, xm_pairs, og_pairs, om_pairs,
    ):
        for send, _ in pairs:
            send().wait_send()

    for which in range(2):

        @pl.when(quad < 2)
        def _():
            b_next(which).wait_send()

        @pl.when(quad == 1)
        def _():
            b_skip(which).wait_send()

        @pl.when(quad == 2)
        def _():
            b_sum(which).wait_send()

    for d in range(1, NH):
        w_send(d).wait_send()
    y_copy(me, mate).wait_send()
    for slot in far:
        y_copy(me, slot).wait_send()
        y_on(slot).wait_send()


def local(q, k, v, fg, counts, gs, ms, ridge, gain, ow):
    vmem = pl.BlockSpec(memory_space=pltpu.VMEM)
    hbm = pl.BlockSpec(memory_space=pltpu.HBM)
    V, DMA = pltpu.VMEM, pltpu.SemaphoreType.DMA
    return pl.pallas_call(
        kernel,
        out_shape=jax.ShapeDtypeStruct((T, 2 * DH), BF16),
        in_specs=[hbm] * 10,
        out_specs=vmem,
        scratch_shapes=[
            pltpu.SMEM((1,), jnp.int32),
            V((2, DH), F32),
            V((2, DH), F32),
            V((T, 2 * DH), BF16),
            V((T, 2 * DH), BF16),
            V((T, 2 * DH), BF16),
            V((2, T), F32),
            V((4, DH, DH), F32),
            V((NG, 32, DH), BF16),
            V((NG, 32, DH), BF16),
            V((NG, 16, DH), BF16),
            V((NG, 16, DH), BF16),
            V((2, NG, 16, DH), F32),
            V((2, 16, DH), F32),
            V((2, 16, DH), F32),
            V((2, 24, DH), F32),
            V((2, 24, DH), F32),
            V((NG, 16, DH), BF16),
            V((NG, 16, DH), BF16),
            V((NG, 16, DH), BF16),
            V((NG, 16, DH), BF16),
            V((2, T + DH, 2 * DH), BF16),
            V((2, DH, 2 * T), BF16),
            V((2, DH, T), BF16),
            V((2, T, T), F32),
            V((2, T, T), F32),
            V((2, DH, T), F32),
            V((2, 1, T), F32),
            V((2, DH, T), F32),
            V((2, DH, T), F32),
            V((2, DH, T), F32),
            V((NH, T, 2 * DH), BF16),
            V((NH, T, 2 * DH), BF16),
            V((T, 2 * DH), F32),
            DMA((10,)),
            pltpu.SemaphoreType.REGULAR((2,)),
            DMA((2, 2, NG)),
            DMA((2, 5)),
            DMA((2, 2, NG)),
            DMA((NH,)),
            DMA((NH,)),
            DMA((NH,)),
            DMA((NH,)),
            DMA((NH,)),
        ],
        compiler_params=pltpu.CompilerParams(
            collective_id=0, has_side_effects=True, vmem_limit_bytes=int(53.8 * 1024 * 1024)
        ),
        cost_estimate=pl.CostEstimate(
            flops=3_000_000_000, bytes_accessed=2_500_000, transcendentals=300_000
        ),
        name="mesa_layer",
    )(counts, q, k, v, fg.T, gs, ms, ridge, gain.reshape(2, DH), ow)


def solution(mesh):
    return jax.shard_map(
        local,
        mesh=mesh,
        in_specs=(
            P("seq", "head"),
            P("seq", "head"),
            P("seq", "head"),
            P("seq", "head"),
            P("seq"),
            P("head", None, None),
            P("head", None, None),
            P("head", None),
            P("head"),
            P("head", None),
        ),
        out_specs=P("seq", "head"),
        check_vma=False,
    )
```

```python
import jax
import jax.numpy as jnp
from jax import lax
from jax.experimental import pallas as pl
from jax.experimental.pallas import tpu as pltpu
from jax.sharding import PartitionSpec as P

ITERS = 16
EARLY = 4
NQ, NG, NX, NH = 4, 16, 4, 8
T, DH = 256, 128
MESH = pl.DeviceIdType.MESH
F32, BF16 = jnp.float32, jnp.bfloat16


def dot(a, b):
    return jnp.dot(a, b, preferred_element_type=F32)


def two_parts(a):
    hi = a.astype(BF16)
    return hi, (a - hi.astype(F32)).astype(BF16)


def three_parts(a):
    hi = a.astype(BF16).astype(F32)
    mid = (a - hi).astype(BF16).astype(F32)
    return hi, mid, a - hi - mid


def kernel(
    cnt_ref, q_hbm, k_hbm, v_hbm, fg, gs_hbm, ms_hbm, rd_ref, ng_ref, ow_hbm, out_ref,
    qv, kv, vv, st,
    xs, xr, xsm, xrm, part, bs, br, bt, bu, xo, xg, xom, xgm,
    kg, kt, vt, wk, wv, rb, lead_s, x_s, r_s, p_s,
    wcol, yg, acc_s,
    lsem, ready, x_sem, b_sem, o_sem, w_s, w_r, y_s, y_r, f_s,
):
    seq = lax.axis_index("seq")
    me = lax.axis_index("head")
    quad, mine = lax.div(seq, NG), lax.rem(seq, NG)

    def peer(dz, dx):
        other = lax.rem(lax.div(mine, NX) + dz, NX) * NX + lax.rem(lax.rem(mine, NX) + dx, NX)
        return other, quad * NG + other

    steps = [(dz, dx) for dz in (2, 3, 1, 0) for dx in (2, 1, 3, 0)][:-1]

    above, below = seq + NG, seq - NG

    loads = [
        pltpu.make_async_copy(k_hbm, kv, lsem.at[1]),
        pltpu.make_async_copy(v_hbm, vv, lsem.at[2]),
        pltpu.make_async_copy(q_hbm, qv, lsem.at[3]),
        pltpu.make_async_copy(gs_hbm, st.at[pl.ds(0, 2)], lsem.at[4]),
        pltpu.make_async_copy(ms_hbm, st.at[pl.ds(2, 2)], lsem.at[5]),
    ]
    for c in loads:
        c.start()
    w_own = pltpu.make_async_copy(
        ow_hbm.at[:, pl.ds(pl.multiple_of(me * T, T), T)], wcol.at[me], lsem.at[6]
    )
    w_own.start()

    barrier = pltpu.get_barrier_semaphore()
    for dz, dx in steps:
        pl.semaphore_signal(barrier, inc=1, device_id=(peer(dz, dx)[1], me), device_id_type=MESH)
    for d in range(1, NH):
        pl.semaphore_signal(
            barrier, inc=1, device_id=(seq, lax.rem(me + d, NH)), device_id_type=MESH
        )

    @pl.when(quad < NQ - 1)
    def _():
        pl.semaphore_signal(barrier, inc=1, device_id=(above, me), device_id_type=MESH)

    @pl.when(quad == 1)
    def _():
        pl.semaphore_signal(barrier, inc=1, device_id=(seq + 2 * NG, me), device_id_type=MESH)

    @pl.when(quad == 3)
    def _():
        pl.semaphore_wait(barrier, NG + NH)
        pl.semaphore_signal(ready.at[1], inc=1, device_id=(seq - 2 * NG, me), device_id_type=MESH)
        pl.semaphore_signal(ready.at[0], inc=1, device_id=(below, me), device_id_type=MESH)

    count = cnt_ref[0]
    live_col = (lax.broadcasted_iota(jnp.int32, (T, 1), 0) < count).astype(F32)
    live_row = (lax.broadcasted_iota(jnp.int32, (1, T), 1) < count).astype(F32)
    logs = jnp.where(live_row > 0, jnp.log(fg[...]), 0.0)
    rows8 = jnp.concatenate([logs, jnp.zeros((6, T), F32)], axis=0)
    stacked = jnp.concatenate([*three_parts(rows8), jnp.zeros_like(rows8)], axis=0).astype(BF16)
    si = lax.broadcasted_iota(jnp.int32, (T, T + DH), 0)
    ti = lax.broadcasted_iota(jnp.int32, (T, T + DH), 1)
    upto = jnp.where(si <= ti, 1.0, 0.0).astype(BF16)
    sums = dot(stacked, upto)
    sums = sums[0:8] + sums[8:16] + sums[16:24]
    run_row, tot = sums[:, 0:T], sums[:, T:]
    run_col = jnp.concatenate([run_row, jnp.zeros((DH - 8, T), F32)], axis=0).T

    loads[0].wait()
    scale = []
    weighted = []
    own = []
    for h in range(2):
        cols = slice(h * DH, (h + 1) * DH)
        kb = kv[:, cols]
        kf = kb.astype(F32)
        sc = lax.rsqrt(jnp.sum(kf * kf, axis=1, keepdims=True) + 1e-06) * live_col
        scale.append(sc)
        wm = kf * (jnp.exp(tot[h : h + 1, 0:1] - run_col[:, h : h + 1]) * sc)
        weighted.append(wm)
        wg_hi, wg_lo = two_parts(wm * sc)
        ktr = kf.T.astype(BF16)
        kt[h] = jnp.concatenate([ktr, ktr], axis=1)
        kg[h, 0:T] = jnp.concatenate([kb, kb], axis=1)
        own.append(dot(ktr, wg_hi) + dot(ktr, wg_lo))
    for j in range(NG):
        h, at = j // 8, 16 * (j % 8)
        xs[j] = jnp.concatenate(
            [own[h][at : at + 16], *three_parts(tot[h : h + 1]), jnp.zeros((13, DH), F32)], axis=0
        ).astype(BF16)

    @pl.when(quad < 3)
    def _():
        pl.semaphore_wait(barrier, NG + NH - 2 + jnp.minimum(quad, 1))


    def swap(src, dst, sem, pair, to, here):
        def send():
            return pltpu.make_async_remote_copy(
                src.at[to], dst.at[here], sem.at[0, to], sem.at[1, here],
                device_id=(pair, me), device_id_type=MESH,
            )

        def come():
            return pltpu.make_async_remote_copy(
                dst.at[to], dst.at[to], sem.at[0, to], sem.at[1, to],
                device_id=(pair, me), device_id_type=MESH,
            )

        return send, come

    def around(src, dst, sem):
        return [swap(src, dst, sem, dev, other, mine) for other, dev in (peer(*d) for d in steps)]

    def start(pairs):
        for send, _ in pairs:
            send().start()

    def arrive(pairs):
        for _, come in reversed(pairs):
            come().wait_recv()

    xg_pairs, xm_pairs = around(xs, xr, x_sem.at[0]), around(xsm, xrm, x_sem.at[1])
    start(xg_pairs)


    @pl.when((quad > 0) & (quad < 3))
    def _():
        pl.semaphore_signal(ready.at[0], inc=1, device_id=(below, me), device_id_type=MESH)

    xr[mine] = xs[mine]
    loads[1].wait()
    own = []
    for h in range(2):
        cols = slice(h * DH, (h + 1) * DH)
        wm_hi, wm_lo = two_parts(weighted[h])
        vtr = vv[:, cols].astype(F32).T.astype(BF16)
        vt[h] = vtr
        own.append(dot(vtr, wm_hi) + dot(vtr, wm_lo))
    for j in range(NG):
        at = 16 * (j % 8)
        xsm[j] = own[j // 8][at : at + 16].astype(BF16)
    start(xm_pairs)
    xrm[mine] = xsm[mine]

    def w_send(d):
        ph = lax.rem(me + d, NH)
        return pltpu.make_async_remote_copy(
            ow_hbm.at[:, pl.ds(pl.multiple_of(ph * T, T), T)],
            wcol.at[me],
            w_s.at[ph],
            w_r.at[me],
            device_id=(seq, ph),
            device_id_type=MESH,
        )

    def w_come(d):
        ph = lax.rem(me + d, NH)
        return pltpu.make_async_remote_copy(
            wcol.at[ph], wcol.at[ph], w_s.at[ph], w_r.at[ph], device_id=(seq, ph), device_id_type=MESH
        )

    for d in range(1, NH):
        w_send(d).start()

    loads[2].wait()
    rr0 = []
    for h in range(2):
        cols = slice(h * DH, (h + 1) * DH)
        decayed = jnp.where(
            si[:, 0:T] <= ti[:, 0:T],
            jnp.exp(jnp.minimum(run_row[h : h + 1] - run_col[:, h : h + 1], 0.0)),
            0.0,
        )
        wv_h = decayed * scale[h]
        wv[h] = wv_h
        wk[h] = wv_h * scale[h]
        lead_s[h] = jnp.exp(run_row[h : h + 1])
        ridge = jnp.broadcast_to(rd_ref[h : h + 1, :], (DH, DH)).T
        rb[h] = jnp.concatenate([ridge, ridge], axis=1)
        qt = qv[:, cols].astype(F32).T
        qn = qt * lax.rsqrt(jnp.sum(qt * qt, axis=0, keepdims=True) + 1e-06)
        x_s[h] = jnp.zeros_like(qn)
        r_s[h] = qn
        p_s[h] = qn
        rr0.append(jnp.sum(qn * qn, axis=0, keepdims=True))

    def log_in(tail):
        tail = tail.astype(F32)
        return tail[0:1] + tail[1:2] + tail[2:3]

    def b_copy(which, n, to):
        src, dst = (bt, bu) if n == 2 else (bs, br)
        return pltpu.make_async_remote_copy(
            src.at[which], dst.at[which], b_sem.at[which, n], b_sem.at[which, 3 + n // 2],
            device_id=(to, me), device_id_type=MESH,
        )

    def b_next(which):
        return b_copy(which, 0, above)

    def b_skip(which):
        return b_copy(which, 1, seq + 2 * NG)

    def b_sum(which):
        return b_copy(which, 2, above)

    def in_quad(which, got):
        run = jnp.zeros((16, DH), F32)
        for k in range(NG):
            part[which, k] = run
            run = jnp.exp(logs[k]) * run + got[k, 0:16].astype(F32)
        return run

    head = lax.div(mine, 8)
    begin_row = pl.multiple_of(16 * lax.rem(mine, 8), 16)

    arrive(xg_pairs)
    logs = [log_in(xr[k, 16:32]) for k in range(NG)]
    lead_in = [jnp.zeros((1, DH), F32)]
    for k in range(NG):
        lead_in.append(lead_in[k] + logs[k])
    loads[3].wait()
    loads[4].wait()
    starts = (st[head, pl.ds(begin_row, 16), :], st[2 + head, pl.ds(begin_row, 16), :])

    def pass_sum(which, total):
        @pl.when(quad == 0)
        def _():
            br[which] = starts[which]

        @pl.when(quad == 2)
        def _():
            bt[which, 0:16] = total
            bt[which, 16:24] = jnp.broadcast_to(lead_in[NG], (8, DH))
            if which == 0:
                pl.semaphore_wait(ready.at[0], 1)
            b_sum(which).start()

    def pass_outcome(which, total):
        @pl.when(quad == 1)
        def _():
            b_next(which).wait_recv()

        @pl.when(quad < 2)
        def _():
            bs[which] = jnp.exp(lead_in[NG]) * br[which] + total
            if which == 0:
                pl.semaphore_wait(ready.at[0], 1)
            b_next(which).start()

        @pl.when(quad == 1)
        def _():
            if which == 0:
                pl.semaphore_wait(ready.at[1], 1)
            b_skip(which).start()

    def take_in(which):
        @pl.when(quad > 1)
        def _():
            b_next(which).wait_recv()

        @pl.when(quad == 3)
        def _():
            b_sum(which).wait_recv()
            br[which] = jnp.exp(bu[which, 16:17]) * br[which] + bu[which, 0:16]

        return br[which]

    def finish(which, carry, out):
        for k in range(NG):
            out[k] = (jnp.exp(lead_in[k]) * carry + part[which, k]).astype(BF16)

    total = in_quad(0, xr)
    pass_sum(0, total)
    pass_outcome(0, total)
    carry = take_in(0)
    finish(0, carry, xo)
    og_pairs, om_pairs = around(xo, xg, o_sem.at[0]), around(xom, xgm, o_sem.at[1])
    start(og_pairs)
    xg[mine] = xo[mine]

    arrive(xm_pairs)
    total = in_quad(1, xrm)
    pass_sum(1, total)
    pass_outcome(1, total)

    arrive(og_pairs)
    for h in range(2):
        g = xg[8 * h : 8 * h + 8].reshape(DH, DH)
        kg[h, T:] = jnp.concatenate([g, g], axis=1)

    def step(i, norms):
        ps = [p_s[h] for h in range(2)]
        us = [dot(kg[h], jnp.concatenate(two_parts(ps[h]), axis=0)) for h in range(2)]
        nears = [jnp.concatenate(two_parts(us[h][0:T] * wk[h]), axis=0) for h in range(2)]
        ws = [dot(kt[h], nears[h]) for h in range(2)]
        ws = [ws[h] + (lead_s[h] * us[h][T:] + rb[h] * ps[h]) for h in range(2)]
        alphas = [norms[h] / jnp.sum(ps[h] * ws[h], axis=0, keepdims=True) for h in range(2)]
        after = []
        for h in range(2):
            x_s[h] += alphas[h] * ps[h]
            r = r_s[h] - alphas[h] * ws[h]
            r_s[h] = r
            new = jnp.sum(r * r, axis=0, keepdims=True)
            p_s[h] = r + (new / norms[h]) * ps[h]
            after.append(new)
        return tuple(after)

    norms = lax.fori_loop(0, EARLY, step, tuple(rr0), unroll=2)
    finish(1, take_in(1), xom)
    start(om_pairs)
    xgm[mine] = xom[mine]
    lax.fori_loop(EARLY, ITERS, step, norms, unroll=2)
    arrive(om_pairs)

    ys = []
    for h in range(2):
        xb = x_s[h].astype(BF16)
        mem = xgm[8 * h : 8 * h + 8].reshape(DH, DH)
        near = (dot(kg[h, 0:T, 0:DH], xb) * wv[h]).astype(BF16)
        o = dot(vt[h], near) + lead_s[h] * dot(mem, xb)
        o = o * (lax.rsqrt(jnp.mean(o * o, axis=0, keepdims=True) + 1e-05) * live_row)
        ys.append(o.T * ng_ref[h : h + 1, :])
    yg[me] = jnp.concatenate(ys, axis=1).astype(BF16)

    mate = me + 1 - 2 * lax.rem(me, 2)

    def y_copy(slot, to):
        return pltpu.make_async_remote_copy(
            yg.at[slot], yg.at[slot], y_s.at[to], y_r.at[slot], device_id=(seq, to), device_id_type=MESH
        )

    def y_on(slot):
        return pltpu.make_async_remote_copy(
            yg.at[slot], yg.at[slot], f_s.at[slot], y_r.at[slot], device_id=(seq, mate), device_id_type=MESH
        )

    far = [lax.rem(me + d, NH) for d in (4, 2, 6)]
    for to in far:
        y_copy(me, to).start()
    y_copy(me, mate).start()
    w_own.wait()
    for d in range(1, NH):
        w_come(d).wait_recv()

    def product(slot):
        return dot(yg[slot], wcol[slot]).astype(BF16).astype(F32)

    acc = product(me)
    y_copy(mate, mate).wait_recv()
    acc = acc + product(mate)
    order = [far[1], far[2], far[0]]
    for slot in order:
        y_copy(slot, slot).wait_recv()
        y_on(slot).start()
        acc = acc + product(slot)
    for slot in order:
        other = slot + mate - me
        y_copy(other, mate).wait_recv()
        acc = acc + product(other)
    out_ref[...] = acc.astype(BF16)

    for pairs in (
        xg_pairs, xm_pairs, og_pairs, om_pairs,
    ):
        for send, _ in pairs:
            send().wait_send()

    for which in range(2):

        @pl.when(quad < 2)
        def _():
            b_next(which).wait_send()

        @pl.when(quad == 1)
        def _():
            b_skip(which).wait_send()

        @pl.when(quad == 2)
        def _():
            b_sum(which).wait_send()

    for d in range(1, NH):
        w_send(d).wait_send()
    y_copy(me, mate).wait_send()
    for slot in far:
        y_copy(me, slot).wait_send()
        y_on(slot).wait_send()


def local(q, k, v, fg, counts, gs, ms, ridge, gain, ow):
    vmem = pl.BlockSpec(memory_space=pltpu.VMEM)
    hbm = pl.BlockSpec(memory_space=pltpu.HBM)
    smem = pl.BlockSpec(memory_space=pltpu.SMEM)
    V, DMA = pltpu.VMEM, pltpu.SemaphoreType.DMA
    return pl.pallas_call(
        kernel,
        out_shape=jax.ShapeDtypeStruct((T, 2 * DH), BF16),
        in_specs=[smem, hbm, hbm, hbm, vmem, hbm, hbm, vmem, vmem, hbm],
        out_specs=vmem,
        scratch_shapes=[
            V((T, 2 * DH), BF16),
            V((T, 2 * DH), BF16),
            V((T, 2 * DH), BF16),
            V((4, DH, DH), F32),
            V((NG, 32, DH), BF16),
            V((NG, 32, DH), BF16),
            V((NG, 16, DH), BF16),
            V((NG, 16, DH), BF16),
            V((2, NG, 16, DH), F32),
            V((2, 16, DH), F32),
            V((2, 16, DH), F32),
            V((2, 24, DH), F32),
            V((2, 24, DH), F32),
            V((NG, 16, DH), BF16),
            V((NG, 16, DH), BF16),
            V((NG, 16, DH), BF16),
            V((NG, 16, DH), BF16),
            V((2, T + DH, 2 * DH), BF16),
            V((2, DH, 2 * T), BF16),
            V((2, DH, T), BF16),
            V((2, T, T), F32),
            V((2, T, T), F32),
            V((2, DH, T), F32),
            V((2, 1, T), F32),
            V((2, DH, T), F32),
            V((2, DH, T), F32),
            V((2, DH, T), F32),
            V((NH, T, 2 * DH), BF16),
            V((NH, T, 2 * DH), BF16),
            V((T, 2 * DH), F32),
            DMA((10,)),
            pltpu.SemaphoreType.REGULAR((2,)),
            DMA((2, 2, NG)),
            DMA((2, 5)),
            DMA((2, 2, NG)),
            DMA((NH,)),
            DMA((NH,)),
            DMA((NH,)),
            DMA((NH,)),
            DMA((NH,)),
        ],
        compiler_params=pltpu.CompilerParams(
            collective_id=0, has_side_effects=True, vmem_limit_bytes=int(53.8 * 1024 * 1024)
        ),
        cost_estimate=pl.CostEstimate(
            flops=3_000_000_000, bytes_accessed=2_500_000, transcendentals=300_000
        ),
        name="mesa_layer",
    )(counts, q, k, v, fg.T, gs, ms, ridge, gain.reshape(2, DH), ow)


def solution(mesh):
    return jax.shard_map(
        local,
        mesh=mesh,
        in_specs=(
            P("seq", "head"),
            P("seq", "head"),
            P("seq", "head"),
            P("seq", "head"),
            P("seq"),
            P("head", None, None),
            P("head", None, None),
            P("head", None),
            P("head"),
            P("head", None),
        ),
        out_specs=P("seq", "head"),
        check_vma=False,
    )
```

```python
import jax
import jax.numpy as jnp
from jax import lax
from jax.experimental import pallas as pl
from jax.experimental.pallas import tpu as pltpu
from jax.sharding import PartitionSpec as P

ITERS = 16
EARLY = 4
NQ, NG, NX, NH = 4, 16, 4, 8
T, DH = 256, 128
MESH = pl.DeviceIdType.MESH
F32, BF16 = jnp.float32, jnp.bfloat16


def dot(a, b):
    return jnp.dot(a, b, preferred_element_type=F32)


def two_parts(a):
    hi = a.astype(BF16)
    return hi, (a - hi.astype(F32)).astype(BF16)


def three_parts(a):
    hi = a.astype(BF16).astype(F32)
    mid = (a - hi).astype(BF16).astype(F32)
    return hi, mid, a - hi - mid


def kernel(
    cnt_ref, q_hbm, k_hbm, v_hbm, fg, gs_hbm, ms_hbm, rd_ref, ng_ref, ow_hbm, out_ref,
    qv, kv, vv, st,
    xs, xr, xsm, xrm, part, bs, br, bt, bu, xo, xg, xom, xgm,
    kg, kt, vt, wk, wv, rb, lead_s, x_s, r_s, p_s,
    wcol, yg, acc_s,
    lsem, ready, x_sem, b_sem, o_sem, w_s, w_r, y_s, y_r,
):
    seq = lax.axis_index("seq")
    me = lax.axis_index("head")
    quad, mine = lax.div(seq, NG), lax.rem(seq, NG)

    def peer(dz, dx):
        other = lax.rem(lax.div(mine, NX) + dz, NX) * NX + lax.rem(lax.rem(mine, NX) + dx, NX)
        return other, quad * NG + other

    steps = [(dz, dx) for dz in (2, 3, 1, 0) for dx in (2, 1, 3, 0)][:-1]

    above, below = seq + NG, seq - NG

    loads = [
        pltpu.make_async_copy(k_hbm, kv, lsem.at[1]),
        pltpu.make_async_copy(v_hbm, vv, lsem.at[2]),
        pltpu.make_async_copy(q_hbm, qv, lsem.at[3]),
        pltpu.make_async_copy(gs_hbm, st.at[pl.ds(0, 2)], lsem.at[4]),
        pltpu.make_async_copy(ms_hbm, st.at[pl.ds(2, 2)], lsem.at[5]),
    ]
    for c in loads:
        c.start()
    w_own = pltpu.make_async_copy(
        ow_hbm.at[:, pl.ds(pl.multiple_of(me * T, T), T)], wcol.at[me], lsem.at[6]
    )
    w_own.start()

    barrier = pltpu.get_barrier_semaphore()
    for dz, dx in steps:
        pl.semaphore_signal(barrier, inc=1, device_id=(peer(dz, dx)[1], me), device_id_type=MESH)
    for d in range(1, NH):
        pl.semaphore_signal(
            barrier, inc=1, device_id=(seq, lax.rem(me + d, NH)), device_id_type=MESH
        )

    @pl.when(quad < NQ - 1)
    def _():
        pl.semaphore_signal(barrier, inc=1, device_id=(above, me), device_id_type=MESH)

    @pl.when(quad == 1)
    def _():
        pl.semaphore_signal(barrier, inc=1, device_id=(seq + 2 * NG, me), device_id_type=MESH)

    @pl.when(quad == 3)
    def _():
        pl.semaphore_wait(barrier, NG + NH)
        pl.semaphore_signal(ready.at[1], inc=1, device_id=(seq - 2 * NG, me), device_id_type=MESH)
        pl.semaphore_signal(ready.at[0], inc=1, device_id=(below, me), device_id_type=MESH)

    count = cnt_ref[0]
    live_col = (lax.broadcasted_iota(jnp.int32, (T, 1), 0) < count).astype(F32)
    live_row = (lax.broadcasted_iota(jnp.int32, (1, T), 1) < count).astype(F32)
    logs = jnp.where(live_row > 0, jnp.log(fg[...]), 0.0)
    rows8 = jnp.concatenate([logs, jnp.zeros((6, T), F32)], axis=0)
    stacked = jnp.concatenate([*three_parts(rows8), jnp.zeros_like(rows8)], axis=0).astype(BF16)
    si = lax.broadcasted_iota(jnp.int32, (T, T + DH), 0)
    ti = lax.broadcasted_iota(jnp.int32, (T, T + DH), 1)
    upto = jnp.where(si <= ti, 1.0, 0.0).astype(BF16)
    sums = dot(stacked, upto)
    sums = sums[0:8] + sums[8:16] + sums[16:24]
    run_row, tot = sums[:, 0:T], sums[:, T:]
    run_col = jnp.concatenate([run_row, jnp.zeros((DH - 8, T), F32)], axis=0).T

    loads[0].wait()
    scale = []
    weighted = []
    own = []
    for h in range(2):
        cols = slice(h * DH, (h + 1) * DH)
        kb = kv[:, cols]
        kf = kb.astype(F32)
        sc = lax.rsqrt(jnp.sum(kf * kf, axis=1, keepdims=True) + 1e-06) * live_col
        scale.append(sc)
        wm = kf * (jnp.exp(tot[h : h + 1, 0:1] - run_col[:, h : h + 1]) * sc)
        weighted.append(wm)
        ktr = kf.T.astype(BF16)
        kt[h] = jnp.concatenate([ktr, ktr], axis=1)
        kg[h, 0:T] = jnp.concatenate([kb, kb], axis=1)
        own.append(dot(ktr, (wm * sc).astype(BF16)))
    for j in range(NG):
        h, at = j // 8, 16 * (j % 8)
        xs[j] = jnp.concatenate(
            [own[h][at : at + 16], *three_parts(tot[h : h + 1]), jnp.zeros((13, DH), F32)], axis=0
        ).astype(BF16)

    @pl.when(quad < 3)
    def _():
        pl.semaphore_wait(barrier, NG + NH - 2 + jnp.minimum(quad, 1))


    def swap(src, dst, sem, pair, to, here):
        def send():
            return pltpu.make_async_remote_copy(
                src.at[to], dst.at[here], sem.at[0, to], sem.at[1, here],
                device_id=(pair, me), device_id_type=MESH,
            )

        def come():
            return pltpu.make_async_remote_copy(
                dst.at[to], dst.at[to], sem.at[0, to], sem.at[1, to],
                device_id=(pair, me), device_id_type=MESH,
            )

        return send, come

    def around(src, dst, sem):
        return [swap(src, dst, sem, dev, other, mine) for other, dev in (peer(*d) for d in steps)]

    def start(pairs):
        for send, _ in pairs:
            send().start()

    def arrive(pairs):
        for _, come in reversed(pairs):
            come().wait_recv()

    xg_pairs, xm_pairs = around(xs, xr, x_sem.at[0]), around(xsm, xrm, x_sem.at[1])
    start(xg_pairs)


    @pl.when((quad > 0) & (quad < 3))
    def _():
        pl.semaphore_signal(ready.at[0], inc=1, device_id=(below, me), device_id_type=MESH)

    xr[mine] = xs[mine]
    loads[1].wait()
    own = []
    for h in range(2):
        cols = slice(h * DH, (h + 1) * DH)
        vtr = vv[:, cols].astype(F32).T.astype(BF16)
        vt[h] = vtr
        own.append(dot(vtr, weighted[h].astype(BF16)))
    for j in range(NG):
        at = 16 * (j % 8)
        xsm[j] = own[j // 8][at : at + 16].astype(BF16)
    start(xm_pairs)
    xrm[mine] = xsm[mine]

    def w_send(d):
        ph = lax.rem(me + d, NH)
        return pltpu.make_async_remote_copy(
            ow_hbm.at[:, pl.ds(pl.multiple_of(ph * T, T), T)],
            wcol.at[me],
            w_s.at[ph],
            w_r.at[me],
            device_id=(seq, ph),
            device_id_type=MESH,
        )

    def w_come(d):
        ph = lax.rem(me + d, NH)
        return pltpu.make_async_remote_copy(
            wcol.at[ph], wcol.at[ph], w_s.at[ph], w_r.at[ph], device_id=(seq, ph), device_id_type=MESH
        )

    for d in range(1, NH):
        w_send(d).start()

    loads[2].wait()
    rr0 = []
    for h in range(2):
        cols = slice(h * DH, (h + 1) * DH)
        decayed = jnp.where(
            si[:, 0:T] <= ti[:, 0:T],
            jnp.exp(jnp.minimum(run_row[h : h + 1] - run_col[:, h : h + 1], 0.0)),
            0.0,
        )
        wv_h = decayed * scale[h]
        wv[h] = wv_h
        wk[h] = wv_h * scale[h]
        lead_s[h] = jnp.exp(run_row[h : h + 1])
        ridge = jnp.broadcast_to(rd_ref[h : h + 1, :], (DH, DH)).T
        rb[h] = jnp.concatenate([ridge, ridge], axis=1)
        qt = qv[:, cols].astype(F32).T
        qn = qt * lax.rsqrt(jnp.sum(qt * qt, axis=0, keepdims=True) + 1e-06)
        x_s[h] = jnp.zeros_like(qn)
        r_s[h] = qn
        p_s[h] = qn
        rr0.append(jnp.sum(qn * qn, axis=0, keepdims=True))

    def log_in(tail):
        tail = tail.astype(F32)
        return tail[0:1] + tail[1:2] + tail[2:3]

    def b_copy(which, n, to):
        src, dst = (bt, bu) if n == 2 else (bs, br)
        return pltpu.make_async_remote_copy(
            src.at[which], dst.at[which], b_sem.at[which, n], b_sem.at[which, 3 + n // 2],
            device_id=(to, me), device_id_type=MESH,
        )

    def b_next(which):
        return b_copy(which, 0, above)

    def b_skip(which):
        return b_copy(which, 1, seq + 2 * NG)

    def b_sum(which):
        return b_copy(which, 2, above)

    def in_quad(which, got):
        run = jnp.zeros((16, DH), F32)
        for k in range(NG):
            part[which, k] = run
            run = jnp.exp(logs[k]) * run + got[k, 0:16].astype(F32)
        return run

    head = lax.div(mine, 8)
    begin_row = pl.multiple_of(16 * lax.rem(mine, 8), 16)

    arrive(xg_pairs)
    logs = [log_in(xr[k, 16:32]) for k in range(NG)]
    lead_in = [jnp.zeros((1, DH), F32)]
    for k in range(NG):
        lead_in.append(lead_in[k] + logs[k])
    loads[3].wait()
    loads[4].wait()
    starts = (st[head, pl.ds(begin_row, 16), :], st[2 + head, pl.ds(begin_row, 16), :])

    def pass_sum(which, total):
        @pl.when(quad == 0)
        def _():
            br[which] = starts[which]

        @pl.when(quad == 2)
        def _():
            bt[which, 0:16] = total
            bt[which, 16:24] = jnp.broadcast_to(lead_in[NG], (8, DH))
            if which == 0:
                pl.semaphore_wait(ready.at[0], 1)
            b_sum(which).start()

    def pass_outcome(which, total):
        @pl.when(quad == 1)
        def _():
            b_next(which).wait_recv()

        @pl.when(quad < 2)
        def _():
            bs[which] = jnp.exp(lead_in[NG]) * br[which] + total
            if which == 0:
                pl.semaphore_wait(ready.at[0], 1)
            b_next(which).start()

        @pl.when(quad == 1)
        def _():
            if which == 0:
                pl.semaphore_wait(ready.at[1], 1)
            b_skip(which).start()

    def take_in(which):
        @pl.when(quad > 1)
        def _():
            b_next(which).wait_recv()

        @pl.when(quad == 3)
        def _():
            b_sum(which).wait_recv()
            br[which] = jnp.exp(bu[which, 16:17]) * br[which] + bu[which, 0:16]

        return br[which]

    def finish(which, carry, out):
        for k in range(NG):
            out[k] = (jnp.exp(lead_in[k]) * carry + part[which, k]).astype(BF16)

    total = in_quad(0, xr)
    pass_sum(0, total)
    pass_outcome(0, total)
    carry = take_in(0)
    finish(0, carry, xo)
    og_pairs, om_pairs = around(xo, xg, o_sem.at[0]), around(xom, xgm, o_sem.at[1])
    start(og_pairs)
    xg[mine] = xo[mine]

    arrive(xm_pairs)
    total = in_quad(1, xrm)
    pass_sum(1, total)
    pass_outcome(1, total)

    arrive(og_pairs)
    for h in range(2):
        g = xg[8 * h : 8 * h + 8].reshape(DH, DH)
        kg[h, T:] = jnp.concatenate([g, g], axis=1)

    def step(i, norms):
        ps = [p_s[h] for h in range(2)]
        us = [dot(kg[h], jnp.concatenate(two_parts(ps[h]), axis=0)) for h in range(2)]
        nears = [jnp.concatenate(two_parts(us[h][0:T] * wk[h]), axis=0) for h in range(2)]
        ws = [dot(kt[h], nears[h]) for h in range(2)]
        ws = [ws[h] + (lead_s[h] * us[h][T:] + rb[h] * ps[h]) for h in range(2)]
        alphas = [norms[h] / jnp.sum(ps[h] * ws[h], axis=0, keepdims=True) for h in range(2)]
        after = []
        for h in range(2):
            x_s[h] += alphas[h] * ps[h]
            r = r_s[h] - alphas[h] * ws[h]
            r_s[h] = r
            new = jnp.sum(r * r, axis=0, keepdims=True)
            p_s[h] = r + (new / norms[h]) * ps[h]
            after.append(new)
        return tuple(after)

    norms = lax.fori_loop(0, EARLY, step, tuple(rr0), unroll=2)
    finish(1, take_in(1), xom)
    start(om_pairs)
    xgm[mine] = xom[mine]
    lax.fori_loop(EARLY, ITERS, step, norms, unroll=2)
    arrive(om_pairs)

    mate = me + 1 - 2 * lax.rem(me, 2)
    far = [lax.rem(me + d, NH) for d in (4, 2, 6)]

    def y_copy(h, slot, to, n):
        return pltpu.make_async_remote_copy(
            yg.at[h, slot], yg.at[h, slot], y_s.at[h, n], y_r.at[h, slot],
            device_id=(seq, to), device_id_type=MESH,
        )

    def read_out(h):
        mem = xgm[8 * h : 8 * h + 8].reshape(DH, DH)
        xb = x_s[h].astype(BF16)
        near = (dot(kg[h, 0:T, 0:DH], xb) * wv[h]).astype(BF16)
        o = dot(vt[h], near) + lead_s[h] * dot(mem, xb)
        o = o * (lax.rsqrt(jnp.mean(o * o, axis=0, keepdims=True) + 1e-05) * live_row)
        yg[h, me] = (o.T * ng_ref[h : h + 1, :]).astype(BF16)
        for n, to in enumerate(far):
            y_copy(h, me, to, n).start()
        y_copy(h, me, mate, 3).start()

    read_out(0)
    read_out(1)

    order = [1, 2, 0]
    for n in order:
        y_copy(0, far[n], mate, 4 + n).wait_recv()
        y_copy(0, far[n], mate, 4 + n).start()
    w_own.wait()
    for d in range(1, NH):
        w_come(d).wait_recv()

    def product(slot):
        y = jnp.concatenate([yg[0, slot], yg[1, slot]], axis=1)
        return dot(y, wcol[slot]).astype(BF16).astype(F32)

    acc = product(me)
    for h in range(2):
        y_copy(h, mate, mate, 3).wait_recv()
    acc = acc + product(mate)
    for n in order:
        y_copy(1, far[n], mate, 4 + n).wait_recv()
        y_copy(1, far[n], mate, 4 + n).start()
        acc = acc + product(far[n])
    for n in order:
        other = far[n] + mate - me
        for h in range(2):
            y_copy(h, other, mate, 4 + n).wait_recv()
        acc = acc + product(other)
    out_ref[...] = acc.astype(BF16)

    for pairs in (
        xg_pairs, xm_pairs, og_pairs, om_pairs,
    ):
        for send, _ in pairs:
            send().wait_send()

    for which in range(2):

        @pl.when(quad < 2)
        def _():
            b_next(which).wait_send()

        @pl.when(quad == 1)
        def _():
            b_skip(which).wait_send()

        @pl.when(quad == 2)
        def _():
            b_sum(which).wait_send()

    for d in range(1, NH):
        w_send(d).wait_send()
    for h in range(2):
        for n in range(7):
            y_copy(h, me, mate, n).wait_send()


def local(q, k, v, fg, counts, gs, ms, ridge, gain, ow):
    vmem = pl.BlockSpec(memory_space=pltpu.VMEM)
    hbm = pl.BlockSpec(memory_space=pltpu.HBM)
    smem = pl.BlockSpec(memory_space=pltpu.SMEM)
    V, DMA = pltpu.VMEM, pltpu.SemaphoreType.DMA
    return pl.pallas_call(
        kernel,
        out_shape=jax.ShapeDtypeStruct((T, 2 * DH), BF16),
        in_specs=[smem, hbm, hbm, hbm, vmem, hbm, hbm, vmem, vmem, hbm],
        out_specs=vmem,
        scratch_shapes=[
            V((T, 2 * DH), BF16),
            V((T, 2 * DH), BF16),
            V((T, 2 * DH), BF16),
            V((4, DH, DH), F32),
            V((NG, 32, DH), BF16),
            V((NG, 32, DH), BF16),
            V((NG, 16, DH), BF16),
            V((NG, 16, DH), BF16),
            V((2, NG, 16, DH), F32),
            V((2, 16, DH), F32),
            V((2, 16, DH), F32),
            V((2, 24, DH), F32),
            V((2, 24, DH), F32),
            V((NG, 16, DH), BF16),
            V((NG, 16, DH), BF16),
            V((NG, 16, DH), BF16),
            V((NG, 16, DH), BF16),
            V((2, T + DH, 2 * DH), BF16),
            V((2, DH, 2 * T), BF16),
            V((2, DH, T), BF16),
            V((2, T, T), F32),
            V((2, T, T), F32),
            V((2, DH, T), F32),
            V((2, 1, T), F32),
            V((2, DH, T), F32),
            V((2, DH, T), F32),
            V((2, DH, T), F32),
            V((NH, T, 2 * DH), BF16),
            V((2, NH, T, DH), BF16),
            V((T, 2 * DH), F32),
            DMA((10,)),
            pltpu.SemaphoreType.REGULAR((2,)),
            DMA((2, 2, NG)),
            DMA((2, 5)),
            DMA((2, 2, NG)),
            DMA((NH,)),
            DMA((NH,)),
            DMA((2, 7)),
            DMA((2, NH)),
        ],
        compiler_params=pltpu.CompilerParams(
            collective_id=0, has_side_effects=True, vmem_limit_bytes=int(53.8 * 1024 * 1024)
        ),
        cost_estimate=pl.CostEstimate(
            flops=3_000_000_000, bytes_accessed=2_500_000, transcendentals=300_000
        ),
        name="mesa_layer",
    )(counts, q, k, v, fg.T, gs, ms, ridge, gain.reshape(2, DH), ow)


def solution(mesh):
    return jax.shard_map(
        local,
        mesh=mesh,
        in_specs=(
            P("seq", "head"),
            P("seq", "head"),
            P("seq", "head"),
            P("seq", "head"),
            P("seq"),
            P("head", None, None),
            P("head", None, None),
            P("head", None),
            P("head"),
            P("head", None),
        ),
        out_specs=P("seq", "head"),
        check_vma=False,
    )
```
